256 devices in a mesh: tg: 4 (over x), tile: 64 (over z, y, core).
Axes of the slice: x: 4, y: 4, z: 8, core: 2. Of those that a mesh axis runs over, the one named last changes fastest.
Arguments:
- age_cell: int32 [4, 4194304], P('tg', 'tile'), may hold values from 0 to 127
- dur_cell: int32 [4, 4194304], P('tg', 'tile'), may hold values from 0 to 3
- trans_code: int32 [4, 4194304], P('tg', 'tile'), may hold values from 0 to 15
- age_frac: float32 [4, 4194304], P('tg', 'tile'), may hold values from 0 to 1
- dur_frac: float32 [4, 4194304], P('tg', 'tile'), may hold values from 0 to 1
- exposure: float32 [4, 4194304], P('tg', 'tile'), may hold values from 0.05 to 1
- claims: float32 [4, 4194304], P('tg', 'tile'), may hold values from 0.01 to 1
- block_tile: int32 [4, 32768, 1], P('tg', 'tile'), may hold values from 0 to 63; in each aligned block of 512 rows (0 to 511, 512 to 1023, ..., all dimensions but the last counted through in order) at most 16 rows name the same one
- smooth_age: float32 [64], P('tg'), may hold values from 0.5 to 8
- smooth_dur: float32 [64], P('tg'), may hold values from 0.5 to 8
- credibility: float32 [64], P('tg'), may hold values from 0.2 to 2
Outputs:
- smoothed: float32 [64, 256, 128], P('tg', 'tile')
- residual: float32 [64, 256, 128], P('tg', 'tile')
The draws below stay inside these ranges and needn't reach their ends.
Inputs may be any that keep to these rules, and one draw needn't show every extreme that they name: `block_tile`: among the 512 blocks of one device, no tile is named by more than 16 blocks.
All inputs are finite; a program needn't handle non-finite values.
Results may differ from the reference program's by a relative error of at most 0.0074.
Values sent between devices are 32-bit elements; how exact they have to be, the bound alone decides.
A program may use at most 64 MiB of HBM per device.

```python
import math
import jax
import jax.numpy as jnp
import numpy as np
from jax import lax

TRANS = 64
AGE = 128
DT = 4
ITERS = 4
TR_DEV = 16
DUR = 256
BLOCKS_DEV = 512
RECORDS = 4194304
CAP = 16
N_TG = 4
N_TILE = 64


def touch_ends(result, own_key, smallest, high):
    longest = result.shape.index(max(result.shape))
    spots = []
    for shift in (0, 1):
        where = [jax.random.randint(jax.random.fold_in(own_key, axis), (), 0, length) for axis, length in enumerate(result.shape)]
        where[longest] = (where[longest] + shift) % result.shape[longest]
        spots.append(tuple(where))
    return result.at[spots[0]].set(smallest).at[spots[1]].set(high)


def shard_levels(stream_key, dims, pieces, least, largest):
    factor_of = 1.0
    for dim, shards_of in pieces:
        heights = jax.random.uniform(jax.random.fold_in(jax.random.fold_in(stream_key, 6), dim), (shards_of,), jnp.float32, least / len(pieces), largest / len(pieces))
        factor_of = factor_of * jnp.repeat(jnp.exp(heights), dims[dim] // shards_of).reshape((-1,) + (1,) * (len(dims) - 1 - dim))
    return factor_of


def shared_out(key, own, number, rows, amount, top, most, skew):
    sequence = jax.random.permutation(key, amount)
    crowded, usual = portions_of(amount, rows * top, most, skew, True), portions_of(amount, rows * top, most, skew, False)
    places = jnp.arange(amount)

    def named(tallies, offset_by):
        used = int((tallies > 0).sum())
        fixed = max(1, used // 4)
        moved = fixed + (places - fixed + offset_by * (used - fixed)) % max(1, amount - fixed)
        return jnp.zeros((amount,), jnp.int32).at[sequence[jnp.where(places < fixed, places, moved)]].set(jnp.asarray(tallies, jnp.int32))

    tallies = jnp.where(number % 4 == 0, named(crowded, number // 4), named(usual, number - number // 4 - 1))
    mixed = jax.random.permutation(jax.random.fold_in(own, 3), amount)
    donor, taker = mixed[0:amount // 2 * 2:2], mixed[1:amount // 2 * 2:2]
    margin = jnp.minimum(tallies[donor] - 1, most - tallies[taker]) // 2
    margin = jnp.where((donor == sequence[0]) | (taker == sequence[0]) | (tallies[taker] == 0), 0, jnp.maximum(margin, 0))
    moved = jax.random.randint(jax.random.fold_in(own, 4), (amount // 2,), 0, 1 << 20) % (margin + 1)
    tallies = tallies.at[donor].add(-moved).at[taker].add(moved)
    items = jnp.searchsorted(jnp.cumsum(tallies), jnp.arange(rows * top), side="right").astype(jnp.int32)
    table = items.reshape(top, rows).T
    table = table[jax.random.permutation(jax.random.fold_in(own, 1), rows)]
    offset_by = jax.random.randint(jax.random.fold_in(own, 2), (rows, 1), 0, top)
    return jnp.take_along_axis(table, (jnp.arange(top)[None, :] + offset_by) % top, axis=1)


def portions_of(number_of, total, most, lean, full):
    loads = [(1 << 20) // math.isqrt(rank ** lean) + 1 for rank in range(1, number_of + 1)]
    largest = most if full else min(most, max(-(-total // number_of), total * loads[0] // sum(loads)))
    least = 1 if total - largest >= number_of - 1 else 0
    counts, surplus = [largest] + [least] * (number_of - 1), total - largest - least * (number_of - 1)
    while surplus > 0:
        candidates = [i for i in range(1, number_of) if counts[i] < largest] or [i for i in range(1, number_of) if counts[i] < most]
        mass, budget = sum([loads[i] for i in candidates]), surplus
        for i in candidates:
            extra = min(most - counts[i], max(1, budget * loads[i] // mass), surplus)
            counts[i] = counts[i] + extra
            surplus = surplus - extra
    return np.array(counts)


def setup_inputs(seed: int = 0) -> dict:
    streams_of = jax.random.split(jax.random.key(seed), 12)
    age_cell = touch_ends(jax.random.randint(streams_of[0], (N_TG, RECORDS), 0, AGE), jax.random.fold_in(streams_of[0], 1), 0, AGE - 1).astype(jnp.int32)
    dur_cell = touch_ends(jax.random.randint(streams_of[1], (N_TG, RECORDS), 0, DT), jax.random.fold_in(streams_of[1], 1), 0, DT - 1).astype(jnp.int32)
    trans_code = touch_ends(jax.random.randint(streams_of[2], (N_TG, RECORDS), 0, TR_DEV), jax.random.fold_in(streams_of[2], 1), 0, TR_DEV - 1).astype(jnp.int32)
    age_frac = jnp.clip(1.0 * jax.random.uniform(streams_of[3], (N_TG, RECORDS), jnp.float32) ** shard_levels(streams_of[3], (N_TG, RECORDS), ((0, 4), (1, 64)), -0.2, 0.2), 0.0, 1.0)
    dur_frac = jnp.clip(1.0 * jax.random.uniform(streams_of[4], (N_TG, RECORDS), jnp.float32) ** shard_levels(streams_of[4], (N_TG, RECORDS), ((0, 4), (1, 64)), -0.2, 0.2), 0.0, 1.0)
    exposure = jnp.clip(jnp.exp(math.log(1.0) - 2.9957323 * jax.random.uniform(streams_of[5], (N_TG, RECORDS), jnp.float32) ** shard_levels(streams_of[5], (N_TG, RECORDS), ((0, 4), (1, 64)), -0.2, 0.2)), 0.05, 1.0)
    claims = jnp.clip(jnp.exp(math.log(1.0) - 4.6051702 * jax.random.uniform(streams_of[6], (N_TG, RECORDS), jnp.float32) ** shard_levels(streams_of[6], (N_TG, RECORDS), ((0, 4), (1, 64)), -0.2, 0.2)), 0.01, 1.0)
    block_tile_keys = jax.random.split(jax.random.fold_in(streams_of[7], 1), N_TG * (BLOCKS_DEV * N_TILE) // BLOCKS_DEV)
    block_tile_turns = jax.random.permutation(jax.random.fold_in(streams_of[7], 3), N_TG * (BLOCKS_DEV * N_TILE) // BLOCKS_DEV)
    block_tile = jax.vmap(lambda own, number: shared_out(jax.random.fold_in(streams_of[7], 2), own, number, BLOCKS_DEV, N_TILE, 1, CAP, 2))(block_tile_keys, block_tile_turns).reshape((N_TG, BLOCKS_DEV * N_TILE, 1))
    smooth_age = jnp.clip(jnp.exp(math.log(8.0) - 2.7725887 * jax.random.uniform(streams_of[8], (TRANS,), jnp.float32) ** shard_levels(streams_of[8], (TRANS,), ((0, 4),), -0.2, 0.2)), 0.5, 8.0)
    smooth_dur = jnp.clip(jnp.exp(math.log(8.0) - 2.7725887 * jax.random.uniform(streams_of[9], (TRANS,), jnp.float32) ** shard_levels(streams_of[9], (TRANS,), ((0, 4),), -0.2, 0.2)), 0.5, 8.0)
    credibility = jnp.clip(jnp.exp(math.log(2.0) - 2.3025851 * jax.random.uniform(streams_of[10], (TRANS,), jnp.float32) ** shard_levels(streams_of[10], (TRANS,), ((0, 4),), -0.2, 0.2)), 0.2, 2.0)
    return dict(age_cell=age_cell, dur_cell=dur_cell, trans_code=trans_code, age_frac=age_frac, dur_frac=dur_frac, exposure=exposure, claims=claims, block_tile=block_tile, smooth_age=smooth_age, smooth_dur=smooth_dur, credibility=credibility)


def spline(frac):
    rest = 1.0 - frac
    cube = frac * frac * frac
    return (rest * rest * rest / 6.0, (3.0 * cube - 6.0 * frac * frac + 4.0) / 6.0, (-3.0 * cube + 3.0 * frac * frac + 3.0 * frac + 1.0) / 6.0, cube / 6.0)


def penalty_matrix(padded_grid, axis, first, record_count):
    inner_product = padded_grid.shape[axis] - 2
    def part(array, lower, length):
        return lax.slice_in_dim(array, lower, lower + length, axis=axis)
    differenced_values = part(padded_grid, 0, inner_product) - 2.0 * part(padded_grid, 1, inner_product) + part(padded_grid, 2, inner_product)
    layout = [1] * padded_grid.ndim
    layout[axis] = inner_product
    place_indices = first - 2 + lax.iota(jnp.int32, inner_product).reshape(layout)
    differenced_values = jnp.where((place_indices >= 0) & (place_indices <= record_count - 3), differenced_values, 0.0)
    final_result = inner_product - 2
    return part(differenced_values, 2, final_result) - 2.0 * part(differenced_values, 1, final_result) + part(differenced_values, 0, final_result)


def rounded(value):
    return lax.optimization_barrier(value.astype(jnp.bfloat16)).astype(jnp.float32)


def reference(age_cell, dur_cell, trans_code, age_frac, dur_frac, exposure, claims, block_tile, smooth_age, smooth_dur, credibility):
    tiles = jnp.repeat(block_tile[:, :, 0], 128, axis=1)
    duration = (tiles * DT + dur_cell).reshape(-1)
    transition = (lax.iota(jnp.int32, N_TG)[:, None] * TR_DEV + trans_code).reshape(-1)
    ages = age_cell.reshape(-1)
    age_w = spline(age_frac.reshape(-1))
    dur_w = spline(dur_frac.reshape(-1))
    values = (exposure.reshape(-1), claims.reshape(-1))
    rows_pad = DUR + 3
    cols_pad = AGE + 3
    flat = jnp.zeros((2 * TRANS * rows_pad * cols_pad,), jnp.float32)
    base = (transition * rows_pad + duration) * cols_pad + ages
    for channel in range(2):
        for place_d in range(4):
            left = rounded(dur_w[place_d] * values[channel])
            for place_a in range(4):
                index = channel * TRANS * rows_pad * cols_pad + base + place_d * cols_pad + place_a
                flat = flat.at[index].add(left * rounded(age_w[place_a]))
    grid = flat.reshape(2, TRANS, rows_pad, cols_pad)[:, :, 1:DUR + 1, 1:AGE + 1]
    expo_grid = grid[0]
    claim_grid = grid[1]
    prior = jnp.sum(claim_grid, axis=0) / (1.0 + jnp.sum(expo_grid, axis=0))
    weight_a = smooth_age[:, None, None]
    weight_d = smooth_dur[:, None, None]
    cred = credibility[:, None, None]
    diagonal = expo_grid + cred

    def operate(field):
        along_age = penalty_matrix(jnp.pad(field, ((0, 0), (0, 0), (2, 2))), 2, 0, AGE)
        along_dur = penalty_matrix(jnp.pad(field, ((0, 0), (2, 2), (0, 0))), 1, 0, DUR)
        return diagonal * field + weight_a * along_age + weight_d * along_dur

    right_side = claim_grid + cred * prior[None]
    smoothed = jnp.zeros_like(right_side)
    residual = right_side
    direction = right_side
    norm_now = jnp.sum(residual * residual, axis=(1, 2))
    for turn in range(ITERS):
        image = operate(direction)
        alpha = norm_now / jnp.sum(direction * image, axis=(1, 2))
        smoothed = smoothed + alpha[:, None, None] * direction
        residual = residual - alpha[:, None, None] * image
        norm_next = jnp.sum(residual * residual, axis=(1, 2))
        direction = residual + (norm_next / norm_now)[:, None, None] * direction
        norm_now = norm_next
    return smoothed, residual
```

```python
import jax, jax.numpy as jnp
from jax import lax
from jax.experimental import pallas as pl
from jax.experimental.pallas import tpu as pltpu
from jax.sharding import Mesh
from jax.sharding import PartitionSpec as P

ITERS = 4
MESH = pl.DeviceIdType.MESH
F32, BF16, I32 = jnp.float32, jnp.bfloat16, jnp.int32

def spline(f):
    r = 1.0 - f
    f2 = f * f
    c = f2 * f
    s = 1.0 / 6.0
    return (r * r * r * s, (3.0 * c - 6.0 * f2 + 4.0) * s, (-3.0 * c + 3.0 * f2 + 3.0 * f + 1.0) * s, c * s)

def grid_kernel(tile_ref, age_ref, dur_ref, code_ref, af_ref, df_ref, ex_ref, cl_ref, out_ref, acc):
    acc[...] = jnp.zeros(acc.shape, F32)
    iota8 = lax.broadcasted_iota(I32, (8, 128), 0)
    iota16 = lax.broadcasted_iota(I32, (16, 128), 0)
    half16 = (iota16 >> 3).astype(F32).astype(BF16)
    zero16 = jnp.zeros((16, 128), BF16)
    r1 = iota16 + 1

    def group(g, _):
        base = pl.multiple_of(g * 8, 8)
        at = pl.ds(base, 8)
        aw = spline(af_ref[at, :])
        dw = spline(df_ref[at, :])
        age, dc = age_ref[at, :], dur_ref[at, :]
        code = code_ref[at, :].astype(F32)
        ex, cl = ex_ref[at, :], cl_ref[at, :]
        for i in range(8):
            def row(x, n):
                return jnp.broadcast_to(x[i : i + 1, :], (n, 128))
            delta = iota8 - row(dc, 8)
            w = jnp.where(delta == 0, row(dw[0], 8), 0.0)
            for k in range(1, 4):
                w = jnp.where(delta == k, row(dw[k], 8), w)
            e = w * row(ex, 8)
            c = w * row(cl, 8)
            e16 = jnp.concatenate([e, e], 0).astype(BF16)
            c16 = jnp.concatenate([c, c], 0).astype(BF16)
            code16 = row(code, 16).astype(BF16)
            le, lc = [], []
            rel = code16 - half16
            for j in range(8):
                m = rel == jnp.bfloat16(2 * j)
                le.append(jnp.where(m, e16, zero16))
                lc.append(jnp.where(m, c16, zero16))
            lhs = jnp.concatenate(le + lc, 0)
            ageb = row(age, 16)
            kk = (r1 - ageb) & 15
            a = jnp.where(kk == 0, row(aw[0], 16), 0.0)
            for k in range(1, 4):
                a = jnp.where(kk == k, row(aw[k], 16), a)
            a16 = a.astype(BF16)
            grp = ((ageb - 1 + kk) >> 4).astype(F32).astype(BF16)
            rhs = jnp.concatenate([jnp.where(grp == jnp.bfloat16(q), a16, zero16) for q in range(8)], 0)
            res = lax.dot_general(lhs, rhs, (((1,), (1,)), ((), ())), preferred_element_type=F32)
            tile = tile_ref[g * 8 + i]
            idx = (tile & 1) * 32 + (tile >> 1)
            acc[idx] += res
        return 0

    lax.fori_loop(0, 64, group, 0)

    sub = lax.broadcasted_iota(I32, (8, 128), 0)

    def comb(m, _):
        h = m // 16
        s = (m % 16) // 8
        r8 = pl.multiple_of((m % 8) * 8, 8)
        up = jnp.minimum(m + 1, 31)
        dn = jnp.maximum(m - 1, 0)
        pooled = [jnp.zeros((8, 128), F32), jnp.zeros((8, 128), F32)]
        for ch in range(2):
            for t in range(16):
                ct = ch * 16 + t
                sl = pl.ds(ct * 8, 8)
                ev = jnp.where(sub == 0, acc[up, sl, :], acc[m, sl, :])
                ev = jnp.where((sub == 0) & (m == 31), 0.0, ev)
                ev = pltpu.roll(ev, 7, 0)
                od = jnp.where(sub >= 5, acc[32 + dn, sl, :], acc[32 + m, sl, :])
                od = jnp.where((sub >= 5) & (m == 0), 0.0, od)
                od = pltpu.roll(od, 3, 0)
                v = ev + od
                pooled[ch] = pooled[ch] + v
                z, y = t >> 1, 2 * (t & 1) + s
                slot = jnp.where(h == 0, y * 8 + z, z * 4 + y)
                out_ref[h, slot, pl.ds(ch * 64 + r8, 8), :] = v
        pe, po = pooled
        low = sub < 4
        z, y = m // 4, m % 4
        out_ref[0, y * 8 + z, 128:136, :] = jnp.where(low, pe, pltpu.roll(po, 4, 0))
        out_ref[1, z * 4 + y, 128:136, :] = jnp.where(low, pltpu.roll(pe, 4, 0), po)
        return 0

    lax.fori_loop(0, 32, comb, 0)

def grids(tiles, fields):
    n = pl.BlockSpec(memory_space=pltpu.VMEM)
    return pl.pallas_call(
        grid_kernel,
        out_shape=jax.ShapeDtypeStruct((2, 32, 136, 128), F32),
        in_specs=[pl.BlockSpec(memory_space=pltpu.SMEM)] + [n] * 7,
        out_specs=n,
        scratch_shapes=[pltpu.VMEM((64, 256, 128), F32)],
        compiler_params=pltpu.CompilerParams(vmem_limit_bytes=40 << 20),
        cost_estimate=pl.CostEstimate(flops=2*512*256*128*128, bytes_accessed=6<<20, transcendentals=0),
        name="local_grid",
    )(tiles, *fields)


ROWS = 136


def penalty(v, axis):
    n = v.shape[axis]
    place = lax.broadcasted_iota(I32, v.shape, axis)
    u = v - 2.0 * pltpu.roll(v, n - 1, axis) + pltpu.roll(v, n - 2, axis)
    u = jnp.where(place < n - 2, u, 0.0)
    return u - 2.0 * pltpu.roll(u, 1, axis) + pltpu.roll(u, 2, axis)


def chain_order(n):
    order = [(n // 2, 0)]
    for k in range(n // 2 - 1, 0, -1):
        order += [(k, 1), (k, 0)]
    return order


def reduce_along(n, me, neighbour, piece, land, sizes, send_sem, recv_sem, prepare):
    order = chain_order(n)
    started = []

    def copy(way, j):
        k, first = order[j]
        sub = (0 if first == 0 else 1) if way == 0 else (1 if first == 0 else 0)
        dest = lax.rem(me + (k if way == 0 else n - k), n)
        return dest, sub

    def transfer(way, j):
        dest, sub = copy(way, j)
        return pltpu.make_async_remote_copy(
            src_ref=piece(dest, sub),
            dst_ref=land(way, j, sub),
            send_sem=send_sem.at[way, j],
            recv_sem=recv_sem.at[way, j],
            device_id=neighbour(1 if way == 0 else n - 1),
            device_id_type=MESH,
        )

    def take(way, j, dest):
        _, sub = copy(way, j)
        transfer(way, j).wait_recv()
        target = piece(dest, sub)
        target[...] += land(way, j, sub)[...]

    for j, (k, first) in enumerate(order):
        for way in (0, 1):
            dest, sub = copy(way, j)
            prepare(k, way)
            if (k + 1, first) in order:
                take(way, order.index((k + 1, first)), dest)
            move = transfer(way, j)
            move.start()
            started.append(move)
    prepare(0, 0)
    for first in (1, 0):
        for way in (0, 1):
            take(way, order.index((1, first)), me) if (1, first) in order else None
    return started


def smooth_kernel(
    g_ref, age_weight, dur_weight, credibility, out_s, out_r,
    part, other, land1, land2, grid, pool, twin, prior, done, got,
    local_sem, s0_send, s0_recv, s1_send, s1_recv, s2_send, s2_recv,
    ag_send, ag_recv, x_send, x_recv, t_send, t_recv, y_send, y_recv, z_send, z_recv, o_send, o_recv,
):
    x, z, y, c = (lax.axis_index(a) for a in ("tg", "z", "y", "c"))

    barrier = pltpu.get_barrier_semaphore()

    def greet(i, _):
        zz, yy, cc = i // 8, lax.rem(i // 2, 4), lax.rem(i, 2)

        @pl.when(i != z * 8 + y * 2 + c)
        def _():
            pl.semaphore_signal(barrier, inc=1, device_id=(x, zz, yy, cc), device_id_type=MESH)

        return 0

    lax.fori_loop(0, 64, greet, 0)
    for d in range(1, 4):
        pl.semaphore_signal(barrier, inc=1, device_id=(lax.rem(x + d, 4), z, y, c), device_id_type=MESH)
    pl.semaphore_wait(barrier, 66)

    sibling = (x, z, y, 1 - c)

    def along_y(d):
        return (x, z, lax.rem(y + d, 4), c)

    def along_z(d):
        return (x, lax.rem(z + d, 8), y, c)

    def dests(n, i):
        order = [lax.rem(i + n // 2, n)]
        for k in range(n // 2 - 1, 0, -1):
            order += [lax.rem(i + k, n), lax.rem(i + n - k, n)]
        return order + [i]

    def role(core, n, i, first_axis, n2, i2, second_axis):
        many = 32 // n
        half = many // 2
        sib = 1 - core
        sib_n, sib_i = (8, z) if core == 0 else (4, y)
        sib_many = 32 // sib_n
        sends = []
        for j, d in enumerate(dests(sib_n, sib_i)):
            at = pl.ds(d * sib_many, sib_many)
            move = pltpu.make_async_remote_copy(
                src_ref=g_ref.at[sib, at], dst_ref=other.at[at],
                send_sem=s0_send.at[j], recv_sem=s0_recv.at[j],
                device_id=sibling, device_id_type=MESH,
            )
            move.start()
            sends.append(move)
        mine = []
        for j, d in enumerate(dests(n, i)):
            at = pl.ds(d * many, many)
            load = pltpu.make_async_copy(g_ref.at[core, at], part.at[at], local_sem.at[j])
            load.start()
            mine.append((load, at))
        ready = set()

        def prepare(k, way):
            j = 0 if k == n // 2 else (n - 1 if k == 0 else 1 + 2 * (n // 2 - 1 - k) + way)
            if j in ready:
                return
            ready.add(j)
            load, at = mine[j]
            load.wait()
            pltpu.make_async_remote_copy(
                src_ref=g_ref.at[core, at], dst_ref=other.at[at],
                send_sem=s0_send.at[j], recv_sem=s0_recv.at[j],
                device_id=sibling, device_id_type=MESH,
            ).wait_recv()
            part[at] += other[at]

        def piece1(d, sub):
            return part.at[pl.ds(d * many + sub * half, half)]

        def land_1(way, j, sub):
            return land1.at[pl.ds((way * (n - 1) + j) * half, half)]

        sends += reduce_along(n, i, first_axis, piece1, land_1, None, s1_send, s1_recv, prepare)

        def rows(sub):
            return pl.ds(0, 72) if sub == 0 else pl.ds(72, 64)

        def piece2(d, sub):
            return part.at[i * many + d, rows(sub)]

        def land_2(way, j, sub):
            return land2.at[way * 7 + j, pl.ds(0, 72 if sub == 0 else 64)]

        sends += reduce_along(n2, i2, second_axis, piece2, land_2, None, s2_send, s2_recv, lambda k, way: None)

        own = i * many + i2
        quarter = 2 * c + lax.rem(y, 2)
        for d in range(1, 4):
            move = pltpu.make_async_remote_copy(
                src_ref=part.at[own, pl.ds(128, 8)], dst_ref=pool.at[d],
                send_sem=x_send.at[d], recv_sem=x_recv.at[d],
                device_id=(lax.rem(x + d, 4), z, y, c), device_id_type=MESH,
            )
            move.start()
            sends.append(move)
        pair = y + 1 - 2 * lax.rem(y, 2)
        for j, peer in enumerate(((x, z, y, 1 - c), (x, z, pair, c), (x, z, pair, 1 - c))):
            move = pltpu.make_async_remote_copy(
                src_ref=part.at[own, pl.ds(0, 128)], dst_ref=grid.at[quarter],
                send_sem=ag_send.at[j], recv_sem=ag_recv.at[j],
                device_id=peer, device_id_type=MESH,
            )
            move.start()
            sends.append(move)
        grid[quarter] = part[own, 0:128]
        pool[0] = part[own, 128:136]
        for move in sends:
            move.wait_send()

    @pl.when(c == 0)
    def _():
        role(0, 4, y, along_y, 8, z, along_z)

    @pl.when(c == 1)
    def _():
        role(1, 8, z, along_z, 4, y, along_y)

    def arrive(dst, sem, src=None):
        pltpu.make_async_remote_copy(
            src_ref=dst, dst_ref=dst, send_sem=sem, recv_sem=sem, device_id=sibling, device_id_type=MESH
        ).wait_recv()

    sends = []

    def send(src, dst, s, r, peer):
        move = pltpu.make_async_remote_copy(
            src_ref=src, dst_ref=dst, send_sem=s, recv_sem=r, device_id=peer, device_id_type=MESH
        )
        move.start()
        sends.append(move)

    for d in range(1, 4):
        arrive(pool.at[d], x_recv.at[d])
    total = (pool[0] + pool[1]) + (pool[2] + pool[3])
    twin[0] = pltpu.roll(total, 4, 0) / (1.0 + total)
    send(twin.at[0], twin.at[1], t_send.at[0], t_recv.at[0], sibling)
    arrive(twin.at[1], t_recv.at[0])
    low = jnp.where(c == 0, twin[0], twin[1])
    high = jnp.where(c == 0, twin[1], twin[0])
    under = lax.broadcasted_iota(I32, (8, 128), 0) < 4
    prior[z, y] = jnp.where(under, low, pltpu.roll(high, 4, 0))
    for d in range(1, 4):
        send(prior.at[z, y], prior.at[z, y], y_send.at[d], y_recv.at[d], along_y(d))
    for d in range(1, 4):
        arrive(prior.at[z, lax.rem(y + 4 - d, 4)], y_recv.at[d])
    for d in range(1, 8):
        send(prior.at[z], prior.at[z], z_send.at[d], z_recv.at[d], along_z(d))
    for d in range(1, 8):
        arrive(prior.at[lax.rem(z + 8 - d, 8)], z_recv.at[d])
    quarter = 2 * c + lax.rem(y, 2)
    pair = lax.rem(y, 2)
    for j, q in enumerate((2 * (1 - c) + pair, 2 * c + 1 - pair, 2 * (1 - c) + 1 - pair)):
        arrive(grid.at[q], ag_recv.at[j])

    t = 2 * z + y // 2
    wa, wd, cred = age_weight[t], dur_weight[t], credibility[t]
    expo = jnp.concatenate([grid[q, 0:64] for q in range(4)], 0)
    claim = jnp.concatenate([grid[q, 64:128] for q in range(4)], 0)
    diagonal = expo + cred
    residual = claim + cred * prior[...].reshape(256, 128)
    direction = residual
    smoothed = jnp.zeros_like(residual)

    def dot(a, b):
        return jnp.sum(a * b, axis=(0, 1), keepdims=True)

    norm = dot(residual, residual)
    for _ in range(ITERS):
        image = diagonal * direction + wa * penalty(direction, 1) + wd * penalty(direction, 0)
        alpha = norm / dot(direction, image)
        smoothed = smoothed + alpha * direction
        residual = residual - alpha * image
        new = dot(residual, residual)
        direction = residual + (new / norm) * direction
        norm = new
    done[:, 0] = smoothed.reshape(32, 8, 128)
    done[:, 1] = residual.reshape(32, 8, 128)

    chip = z * 4 + y
    for j in range(16):
        m = quarter * 8 + j // 2
        self_ = (m == chip) & (j % 2 == c)

        @pl.when(jnp.logical_not(self_))
        def _():
            pltpu.make_async_remote_copy(
                src_ref=done.at[m], dst_ref=got.at[t], send_sem=o_send.at[j], recv_sem=o_recv.at[t],
                device_id=(x, m // 4, lax.rem(m, 4), j % 2), device_id_type=MESH,
            ).start()

    mine = z // 2 == quarter

    @pl.when(mine)
    def _():
        got[t] = done[chip]

    for tt in range(16):
        @pl.when(jnp.logical_not(mine & (t == tt)))
        def _():
            arrive(got.at[tt], o_recv.at[tt])

    for tt in range(16):
        for k, out in enumerate((out_s, out_r)):
            v = got[tt, k]
            v = jnp.where(c == 0, v, pltpu.roll(v, 4, 0))
            out[tt] = v[0:4]
    for move in sends:
        move.wait_send()
    for j in range(16):
        m = quarter * 8 + j // 2

        @pl.when(jnp.logical_not((m == chip) & (j % 2 == c)))
        def _():
            pltpu.make_async_remote_copy(
                src_ref=done.at[m], dst_ref=got.at[t], send_sem=o_send.at[j], recv_sem=o_recv.at[t],
                device_id=sibling, device_id_type=MESH,
            ).wait_send()


def smooth(parts, smooth_age, smooth_dur, credibility):
    smem = pl.BlockSpec(memory_space=pltpu.SMEM)
    vmem = pl.BlockSpec(memory_space=pltpu.VMEM)
    dma = pltpu.SemaphoreType.DMA
    return pl.pallas_call(
        smooth_kernel,
        out_shape=(jax.ShapeDtypeStruct((16, 4, 128), F32),) * 2,
        in_specs=[pl.BlockSpec(memory_space=pl.ANY), smem, smem, smem],
        out_specs=(vmem, vmem),
        scratch_shapes=[
            pltpu.VMEM((32, ROWS, 128), F32),
            pltpu.VMEM((32, ROWS, 128), F32),
            pltpu.VMEM((28, ROWS, 128), F32),
            pltpu.VMEM((14, 72, 128), F32),
            pltpu.VMEM((4, 128, 128), F32),
            pltpu.VMEM((4, 8, 128), F32),
            pltpu.VMEM((2, 8, 128), F32),
            pltpu.VMEM((8, 4, 8, 128), F32),
            pltpu.VMEM((32, 2, 8, 128), F32),
            pltpu.VMEM((16, 2, 8, 128), F32),
            dma((8,)), dma((8,)), dma((8,)),
            dma((2, 7)), dma((2, 7)), dma((2, 7)), dma((2, 7)),
            dma((3,)), dma((3,)), dma((4,)), dma((4,)), dma((1,)), dma((1,)),
            dma((4,)), dma((4,)), dma((8,)), dma((8,)), dma((16,)), dma((16,)),
        ],
        compiler_params=pltpu.CompilerParams(collective_id=0, has_side_effects=True, vmem_limit_bytes=40 << 20),
        cost_estimate=pl.CostEstimate(flops=20 << 20, bytes_accessed=6 << 20, transcendentals=0),
        name="reduce_and_smooth",
    )(parts, smooth_age, smooth_dur, credibility)


def per_device(
    age_cell, dur_cell, trans_code, age_frac, dur_frac, exposure, claims, block_tile, smooth_age, smooth_dur, credibility
):
    fields = [
        f.reshape(-1, 128) for f in (age_cell, dur_cell, trans_code, age_frac, dur_frac, exposure, claims)
    ]
    parts = grids(block_tile.reshape(-1), fields)
    return smooth(parts, smooth_age, smooth_dur, credibility)


def solution(mesh):
    split = Mesh(mesh.devices.reshape(mesh.shape["tg"], 8, 4, 2), ("tg", "z", "y", "c"))
    tile = ("z", "y", "c")
    placed = (P("tg", tile),) * 7 + (P("tg", tile, None),) + (P("tg"),) * 3
    return jax.shard_map(
        per_device,
        mesh=split,
        in_specs=placed,
        out_specs=(P("tg", tile, None),) * 2,
        check_vma=False,
    )
```

```python
import jax, jax.numpy as jnp
from jax import lax
from jax.experimental import pallas as pl
from jax.experimental.pallas import tpu as pltpu
from jax.sharding import Mesh
from jax.sharding import PartitionSpec as P

ITERS = 4
MESH = pl.DeviceIdType.MESH
HBM = pltpu.MemorySpace.HBM
F32, BF16, I32 = jnp.float32, jnp.bfloat16, jnp.int32

def spline(f):
    r = 1.0 - f
    f2 = f * f
    c = f2 * f
    s = 1.0 / 6.0
    return (r * r * r * s, (3.0 * c - 6.0 * f2 + 4.0) * s, (-3.0 * c + 3.0 * f2 + 3.0 * f + 1.0) * s, c * s)

def grid_kernel(
    tile_ref, age_hbm, dur_hbm, code_hbm, af_hbm, df_hbm, ex_hbm, cl_hbm, out_ref, pool_ref,
    acc, age_ref, dur_ref, code_ref, af_ref, df_ref, ex_ref, cl_ref, sem,
):
    loads = []
    for part in range(4):
        at = pl.ds(part * 128, 128)
        for k, (src, dst) in enumerate((
            (age_hbm, age_ref), (dur_hbm, dur_ref), (code_hbm, code_ref), (af_hbm, af_ref),
            (df_hbm, df_ref), (ex_hbm, ex_ref), (cl_hbm, cl_ref),
        )):
            loads.append(pltpu.make_async_copy(src.at[at], dst.at[at], sem.at[part, k]))
            loads[-1].start()
    acc[...] = jnp.zeros(acc.shape, F32)
    iota8 = lax.broadcasted_iota(I32, (8, 128), 0)
    iota16 = lax.broadcasted_iota(I32, (16, 128), 0)
    half16 = (iota16 >> 3).astype(F32).astype(BF16)
    zero16 = jnp.zeros((16, 128), BF16)
    r1 = iota16 + 1

    def group(g, _):
        base = pl.multiple_of(g * 8, 8)
        at = pl.ds(base, 8)
        aw = spline(af_ref[at, :])
        dw = spline(df_ref[at, :])
        age, dc = age_ref[at, :], dur_ref[at, :]
        code = code_ref[at, :].astype(F32)
        ex, cl = ex_ref[at, :], cl_ref[at, :]
        for i in range(8):
            def row(x, n):
                return jnp.broadcast_to(x[i : i + 1, :], (n, 128))
            delta = iota8 - row(dc, 8)
            w = jnp.where(delta == 0, row(dw[0], 8), 0.0)
            for k in range(1, 4):
                w = jnp.where(delta == k, row(dw[k], 8), w)
            e = w * row(ex, 8)
            c = w * row(cl, 8)
            e16 = jnp.concatenate([e, e], 0).astype(BF16)
            c16 = jnp.concatenate([c, c], 0).astype(BF16)
            code16 = row(code, 16).astype(BF16)
            le, lc = [], []
            rel = code16 - half16
            for j in range(8):
                m = rel == jnp.bfloat16(2 * j)
                le.append(jnp.where(m, e16, zero16))
                lc.append(jnp.where(m, c16, zero16))
            lhs = jnp.concatenate(le + lc, 0)
            ageb = row(age, 16)
            kk = (r1 - ageb) & 15
            a = jnp.where(kk == 0, row(aw[0], 16), 0.0)
            for k in range(1, 4):
                a = jnp.where(kk == k, row(aw[k], 16), a)
            a16 = a.astype(BF16)
            grp = ((ageb - 1 + kk) >> 4).astype(F32).astype(BF16)
            rhs = jnp.concatenate([jnp.where(grp == jnp.bfloat16(q), a16, zero16) for q in range(8)], 0)
            res = lax.dot_general(lhs, rhs, (((1,), (1,)), ((), ())), preferred_element_type=F32)
            tile = tile_ref[g * 8 + i]
            idx = (tile & 1) * 32 + (tile >> 1)
            acc[idx] += res
        return 0

    for part in range(4):
        for load in loads[part * 7 : part * 7 + 7]:
            load.wait()
        lax.fori_loop(part * 16, part * 16 + 16, group, 0)

    sub = lax.broadcasted_iota(I32, (8, 128), 0)

    def comb(m, _):
        h = m // 16
        s = (m % 16) // 8
        r8 = pl.multiple_of((m % 8) * 8, 8)
        up = jnp.minimum(m + 1, 31)
        dn = jnp.maximum(m - 1, 0)
        pooled = [jnp.zeros((8, 128), F32), jnp.zeros((8, 128), F32)]
        for ch in range(2):
            for t in range(16):
                ct = ch * 16 + t
                sl = pl.ds(ct * 8, 8)
                ev = jnp.where(sub == 0, acc[up, sl, :], acc[m, sl, :])
                ev = jnp.where((sub == 0) & (m == 31), 0.0, ev)
                ev = pltpu.roll(ev, 7, 0)
                od = jnp.where(sub >= 5, acc[32 + dn, sl, :], acc[32 + m, sl, :])
                od = jnp.where((sub >= 5) & (m == 0), 0.0, od)
                od = pltpu.roll(od, 3, 0)
                v = ev + od
                pooled[ch] = pooled[ch] + v
                z, y = t >> 1, 2 * (t & 1) + s
                slot = jnp.where(h == 0, y * 8 + z, z * 4 + y)
                out_ref[h, slot, pl.ds(ch * 64 + r8, 8), :] = v
        pe, po = pooled
        low = sub < 4
        z, y = m // 4, m % 4
        pool_ref[0, y * 8 + z] = jnp.where(low, pe, pltpu.roll(po, 4, 0))
        pool_ref[1, y * 8 + z] = jnp.where(low, pltpu.roll(pe, 4, 0), po)
        return 0

    lax.fori_loop(0, 32, comb, 0)

def grids(tiles, fields):
    vmem = pl.BlockSpec(memory_space=pltpu.VMEM)
    return pl.pallas_call(
        grid_kernel,
        out_shape=(
            jax.ShapeDtypeStruct((2, 32, 128, 128), F32),
            jax.ShapeDtypeStruct((2, 32, 8, 128), F32),
        ),
        in_specs=[pl.BlockSpec(memory_space=pltpu.SMEM)] + [pl.BlockSpec(memory_space=HBM)] * 7,
        out_specs=(vmem, vmem),
        scratch_shapes=[pltpu.VMEM((64, 256, 128), F32)]
        + [pltpu.VMEM((512, 128), I32)] * 3
        + [pltpu.VMEM((512, 128), F32)] * 4
        + [pltpu.SemaphoreType.DMA((4, 7))],
        compiler_params=pltpu.CompilerParams(vmem_limit_bytes=40 << 20),
        cost_estimate=pl.CostEstimate(flops=2 * 512 * 256 * 128 * 128, bytes_accessed=6 << 20, transcendentals=0),
        name="local_grid",
    )(tiles, *fields)


def penalty(v, axis):
    n = v.shape[axis]
    place = lax.broadcasted_iota(I32, v.shape, axis)
    u = v - 2.0 * pltpu.roll(v, n - 1, axis) + pltpu.roll(v, n - 2, axis)
    u = jnp.where(place < n - 2, u, 0.0)
    return u - 2.0 * pltpu.roll(u, 1, axis) + pltpu.roll(u, 2, axis)


def chain_order(n):
    order = [(n // 2, 0)]
    for k in range(n // 2 - 1, 0, -1):
        order += [(k, 1), (k, 0)]
    return order


def reduce_along(n, me, neighbour, piece, land, send_sem, recv_sem, prepare, hook):
    order = chain_order(n)
    started = []

    def half_of(way, j):
        return order[j][1] if way == 0 else 1 - order[j][1]

    def transfer(way, j):
        k, _ = order[j]
        sub = half_of(way, j)
        dest = lax.rem(me + (k if way == 0 else n - k), n)
        return pltpu.make_async_remote_copy(
            src_ref=piece(dest, sub),
            dst_ref=land(way, j),
            send_sem=send_sem.at[way, j],
            recv_sem=recv_sem.at[way, j],
            device_id=neighbour(1 if way == 0 else n - 1),
            device_id_type=MESH,
        )

    def take(way, j, dest):
        transfer(way, j).wait_recv()
        target = piece(dest, half_of(way, j))
        target[...] += land(way, j)[...]

    for j, (k, first) in enumerate(order):
        for way in (0, 1):
            prepare(k, way)
            if (k + 1, first) in order:
                take(way, order.index((k + 1, first)), lax.rem(me + (k if way == 0 else n - k), n))
            move = transfer(way, j)
            move.start()
            started.append(move)
        hook(j)
    prepare(0, 0)
    for first in (1, 0):
        for way in (0, 1):
            take(way, order.index((1, first)), me)
    return started


def smooth_kernel(
    g_ref, p_ref, age_weight, dur_weight, credibility, out_s, out_r,
    part, other, land1, land2, grid, pool_in, pool_part, pool_y, pool_z, pool_zin, pool, twin, prior, field, done, got,
    local_sem, s0_send, s0_recv, s1_send, s1_recv, s2_send, s2_recv, ag_send, ag_recv,
    pa_send, pa_recv, pb_send, pb_recv, pc_send, pc_recv, x_send, x_recv, t_send, t_recv,
    y_send, y_recv, z_send, z_recv, o_send, o_recv,
):
    x, z, y, c = (lax.axis_index(a) for a in ("tg", "z", "y", "c"))
    sibling = (x, z, y, 1 - c)
    side = lax.rem(y, 2)
    pair = y + 1 - 2 * side

    def along_y(d):
        return (x, z, lax.rem(y + d, 4), c)

    def along_z(d):
        return (x, lax.rem(z + d, 8), y, c)

    def along_x(d):
        return (lax.rem(x + d, 4), z, y, c)

    barrier = pltpu.get_barrier_semaphore()
    peers = [sibling, (x, z, pair, 1 - c)]
    peers += [along_y(d) for d in range(1, 4)] + [along_z(d) for d in range(1, 8)] + [along_x(d) for d in range(1, 4)]
    for peer in peers:
        pl.semaphore_signal(barrier, inc=1, device_id=peer, device_id_type=MESH)
    pl.semaphore_wait(barrier, len(peers))

    def dests(n, i):
        order = [lax.rem(i + n // 2, n)]
        for k in range(n // 2 - 1, 0, -1):
            order += [lax.rem(i + k, n), lax.rem(i + n - k, n)]
        return order + [i]

    def arrive(dst, sem):
        pltpu.make_async_remote_copy(
            src_ref=dst, dst_ref=dst, send_sem=sem, recv_sem=sem, device_id=sibling, device_id_type=MESH
        ).wait_recv()

    def role(core, n, i, first_axis, n2, i2, second_axis, points):
        many = 32 // n
        half = many // 2
        sends = []

        def send(src, dst, s, r, peer):
            move = pltpu.make_async_remote_copy(
                src_ref=src, dst_ref=dst, send_sem=s, recv_sem=r, device_id=peer, device_id_type=MESH
            )
            move.start()
            sends.append(move)

        def pool_to_sibling():
            send(p_ref.at[1 - core], pool_in, pa_send.at[0], pa_recv.at[0], sibling)
            own = pltpu.make_async_copy(p_ref.at[core], pool_part, local_sem.at[8])
            own.start()
            return own

        def pool_along_y():
            pool_own.wait()
            arrive(pool_in, pa_recv.at[0])
            pool_part[...] += pool_in[...]
            for d in (2, 1, 3):
                at = pl.ds(lax.rem(y + d, 4) * 8, 8)
                send(pool_part.at[at], pool_y.at[d], pb_send.at[d], pb_recv.at[d], along_y(d))

        def pool_along_z():
            for d in range(1, 4):
                arrive(pool_y.at[d], pb_recv.at[d])
            pool_z[...] = (pool_part[pl.ds(y * 8, 8)] + pool_y[1]) + (pool_y[2] + pool_y[3])
            for d in (4, 3, 5, 2, 6, 1, 7):
                send(pool_z.at[lax.rem(z + d, 8)], pool_zin.at[d], pc_send.at[d], pc_recv.at[d], along_z(d))

        def pool_along_x():
            for d in range(1, 8):
                arrive(pool_zin.at[d], pc_recv.at[d])
            total = pool_z[z]
            for d in range(1, 8):
                total = total + pool_zin[d]
            pool[0] = total
            for d in (2, 1, 3):
                send(pool.at[0], pool.at[d], x_send.at[d], x_recv.at[d], along_x(d))

        def prior_to_sibling():
            for d in range(1, 4):
                arrive(pool.at[d], x_recv.at[d])
            total = (pool[0] + pool[1]) + (pool[2] + pool[3])
            twin[0] = pltpu.roll(total, 4, 0) / (1.0 + total)
            send(twin.at[0], twin.at[1], t_send.at[0], t_recv.at[0], sibling)

        def prior_along_y():
            arrive(twin.at[1], t_recv.at[0])
            low, high = twin[core], twin[1 - core]
            under = lax.broadcasted_iota(I32, (8, 128), 0) < 4
            prior[z, y] = jnp.where(under, low, pltpu.roll(high, 4, 0))
            for d in (2, 1, 3):
                send(prior.at[z, y], prior.at[z, y], y_send.at[d], y_recv.at[d], along_y(d))

        def prior_along_z():
            for d in range(1, 4):
                arrive(prior.at[z, lax.rem(y + 4 - d, 4)], y_recv.at[d])
            for d in (4, 3, 5, 2, 6, 1, 7):
                send(prior.at[z], prior.at[z], z_send.at[d], z_recv.at[d], along_z(d))

        pool_own = pool_to_sibling()
        sib_n, sib_i = (8, z) if core == 0 else (4, y)
        sib_many = 32 // sib_n
        for j, d in enumerate(dests(sib_n, sib_i)):
            at = pl.ds(d * sib_many, sib_many)
            send(g_ref.at[1 - core, at], other.at[at], s0_send.at[j], s0_recv.at[j], sibling)
        mine = []
        for j, d in enumerate(dests(n, i)):
            at = pl.ds(d * many, many)
            load = pltpu.make_async_copy(g_ref.at[core, at], part.at[at], local_sem.at[j])
            load.start()
            mine.append((load, at))
        ready = set()

        def prepare(k, way):
            j = 0 if k == n // 2 else (n - 1 if k == 0 else 1 + 2 * (n // 2 - 1 - k) + way)
            if j in ready:
                return
            ready.add(j)
            load, at = mine[j]
            load.wait()
            arrive(other.at[at], s0_recv.at[j])
            part[at] += other[at]

        def piece(d, sub):
            return part.at[pl.ds(d * many + sub * half, half)]

        def land(way, j):
            return land1.at[pl.ds((way * (n - 1) + j) * half, half)]

        def hook(j):
            if j in points:
                points[j](pool_along_z, pool_along_x, prior_to_sibling)

        pool_along_y()
        sends += reduce_along(n, i, first_axis, piece, land, s1_send, s1_recv, prepare, hook)

        far = sorted(range(1, n2), key=lambda d: -min(d, n2 - d))
        for d in far:
            send(part.at[i * many + lax.rem(i2 + d, n2)], land2.at[d], s2_send.at[d], s2_recv.at[d], second_axis(d))
        prior_along_y()
        quarter = 2 * core + side
        grid[quarter] = part[i * many + i2]
        for d in reversed(far):
            arrive(land2.at[d], s2_recv.at[d])
            grid[quarter] += land2[d]
        for j, peer in enumerate((sibling, (x, z, pair, c), (x, z, pair, 1 - c))):
            send(grid.at[quarter], grid.at[quarter], ag_send.at[j], ag_recv.at[j], peer)
        prior_along_z()
        for d in range(1, 8):
            arrive(prior.at[lax.rem(z + 8 - d, 8)], z_recv.at[d])
        for j, q in enumerate((2 * (1 - core) + side, 2 * core + 1 - side, 2 * (1 - core) + 1 - side)):
            arrive(grid.at[q], ag_recv.at[j])
        for move in sends:
            move.wait_send()

    def nth(k):
        return lambda *steps: steps[k]()

    @pl.when(c == 0)
    def _():
        role(0, 4, y, along_y, 8, z, along_z, {0: nth(0), 1: nth(1), 2: nth(2)})

    @pl.when(c == 1)
    def _():
        role(1, 8, z, along_z, 4, y, along_y, {1: nth(0), 3: nth(1), 5: nth(2)})

    quarter = 2 * c + side
    t = 2 * z + y // 2
    wa, wd, cred = age_weight[t], dur_weight[t], credibility[t]
    expo = jnp.concatenate([grid[q, 0:64] for q in range(4)], 0)
    claim = jnp.concatenate([grid[q, 64:128] for q in range(4)], 0)
    diagonal = expo + cred
    residual = claim + cred * prior[...].reshape(256, 128)
    direction = residual
    smoothed = jnp.zeros_like(residual)

    def dot(a, b):
        return jnp.sum(a * b, axis=(0, 1), keepdims=True)

    norm = dot(residual, residual)
    for _ in range(ITERS):
        image = diagonal * direction + wa * penalty(direction, 1) + wd * penalty(direction, 0)
        alpha = norm / dot(direction, image)
        smoothed = smoothed + alpha * direction
        residual = residual - alpha * image
        new = dot(residual, residual)
        direction = residual + (new / norm) * direction
        norm = new
    field[0] = smoothed
    field[1] = residual

    for j in range(8):
        at = pl.ds(pl.multiple_of(quarter * 64 + j * 8, 8), 8)
        for k in range(2):
            v = field[k, at]
            done[2 * j, k] = v[0:4]
            done[2 * j + 1, k] = v[4:8]

    chip = z * 4 + y

    def result(j):
        m = quarter * 8 + j // 2
        return jnp.logical_not((m == chip) & (j % 2 == c)), pltpu.make_async_remote_copy(
            src_ref=done.at[j], dst_ref=got.at[t], send_sem=o_send.at[j], recv_sem=o_recv.at[t],
            device_id=(x, quarter * 2 + j // 8, (j // 2) % 4, j % 2), device_id_type=MESH,
        )

    for j in range(16):
        away, move = result(j)
        pl.when(away)(move.start)
    here = z // 2 == quarter

    @pl.when(here)
    def _():
        got[t] = done[lax.rem(chip, 8) * 2 + c]

    for tt in range(16):
        @pl.when(jnp.logical_not(here & (t == tt)))
        def _():
            arrive(got.at[tt], o_recv.at[tt])

    out_s[...] = got[:, 0]
    out_r[...] = got[:, 1]
    for j in range(16):
        away, move = result(j)
        pl.when(away)(move.wait_send)


def smooth(parts, pooled, smooth_age, smooth_dur, credibility):
    smem = pl.BlockSpec(memory_space=pltpu.SMEM)
    vmem = pl.BlockSpec(memory_space=pltpu.VMEM)
    whole = pl.BlockSpec(memory_space=pl.ANY)
    dma = pltpu.SemaphoreType.DMA
    return pl.pallas_call(
        smooth_kernel,
        out_shape=(jax.ShapeDtypeStruct((16, 4, 128), F32),) * 2,
        in_specs=[whole, whole, smem, smem, smem],
        out_specs=(vmem, vmem),
        scratch_shapes=[
            pltpu.VMEM((32, 128, 128), F32),
            pltpu.VMEM((32, 128, 128), F32),
            pltpu.VMEM((28, 128, 128), F32),
            pltpu.VMEM((8, 128, 128), F32),
            pltpu.VMEM((4, 128, 128), F32),
            pltpu.VMEM((32, 8, 128), F32),
            pltpu.VMEM((32, 8, 128), F32),
            pltpu.VMEM((4, 8, 8, 128), F32),
            pltpu.VMEM((8, 8, 128), F32),
            pltpu.VMEM((8, 8, 128), F32),
            pltpu.VMEM((4, 8, 128), F32),
            pltpu.VMEM((2, 8, 128), F32),
            pltpu.VMEM((8, 4, 8, 128), F32),
            pltpu.VMEM((2, 256, 128), F32),
            pltpu.VMEM((16, 2, 4, 128), F32),
            pltpu.VMEM((16, 2, 4, 128), F32),
            dma((9,)), dma((8,)), dma((8,)),
            dma((2, 7)), dma((2, 7)), dma((8,)), dma((8,)), dma((3,)), dma((3,)),
            dma((1,)), dma((1,)), dma((4,)), dma((4,)), dma((8,)), dma((8,)),
            dma((4,)), dma((4,)), dma((1,)), dma((1,)),
            dma((4,)), dma((4,)), dma((8,)), dma((8,)), dma((16,)), dma((16,)),
        ],
        compiler_params=pltpu.CompilerParams(collective_id=0, has_side_effects=True, vmem_limit_bytes=40 << 20),
        cost_estimate=pl.CostEstimate(flops=20 << 20, bytes_accessed=6 << 20, transcendentals=0),
        name="reduce_and_smooth",
    )(parts, pooled, smooth_age, smooth_dur, credibility)


def per_device(
    age_cell, dur_cell, trans_code, age_frac, dur_frac, exposure, claims, block_tile, smooth_age, smooth_dur, credibility
):
    fields = [
        f.reshape(-1, 128) for f in (age_cell, dur_cell, trans_code, age_frac, dur_frac, exposure, claims)
    ]
    parts, pooled = grids(block_tile.reshape(-1), fields)
    return smooth(parts, pooled, smooth_age, smooth_dur, credibility)


def solution(mesh):
    split = Mesh(mesh.devices.reshape(mesh.shape["tg"], 8, 4, 2), ("tg", "z", "y", "c"))
    tile = ("z", "y", "c")
    placed = (P("tg", tile),) * 7 + (P("tg", tile, None),) + (P("tg"),) * 3
    return jax.shard_map(
        per_device,
        mesh=split,
        in_specs=placed,
        out_specs=(P("tg", tile, None),) * 2,
        check_vma=False,
    )
```

```python
import jax, jax.numpy as jnp
from jax import lax
from jax.experimental import pallas as pl
from jax.experimental.pallas import tpu as pltpu
from jax.sharding import Mesh
from jax.sharding import PartitionSpec as P

ITERS = 4
MESH = pl.DeviceIdType.MESH
HBM = pltpu.MemorySpace.HBM
F32, BF16, I32 = jnp.float32, jnp.bfloat16, jnp.int32

def spline(f):
    r = 1.0 - f
    f2 = f * f
    c = f2 * f
    s = 1.0 / 6.0
    return (r * r * r * s, (3.0 * c - 6.0 * f2 + 4.0) * s, (-3.0 * c + 3.0 * f2 + 3.0 * f + 1.0) * s, c * s)

def grid_kernel(
    tile_ref, age_hbm, dur_hbm, code_hbm, af_hbm, df_hbm, ex_hbm, cl_hbm, out_hbm, pool_hbm,
    acc, age_ref, dur_ref, code_ref, af_ref, df_ref, ex_ref, cl_ref, weights, out_ref, pool_ref, sem, out_sem,
):
    pairs = (
        (age_hbm, age_ref), (dur_hbm, dur_ref), (code_hbm, code_ref), (af_hbm, af_ref),
        (df_hbm, df_ref), (ex_hbm, ex_ref), (cl_hbm, cl_ref),
    )

    def loads(part):
        at = pl.ds(part * 128, 128)
        return [pltpu.make_async_copy(src.at[at], dst.at[at], sem.at[part, k]) for k, (src, dst) in enumerate(pairs)]

    for part in range(4):
        for load in loads(part):
            load.start()
    acc[...] = jnp.zeros(acc.shape, F32)
    iota8 = lax.broadcasted_iota(I32, (8, 128), 0)
    iota16 = lax.broadcasted_iota(I32, (16, 128), 0)
    half16 = (iota16 >> 3).astype(F32).astype(BF16)
    zero16 = jnp.zeros((16, 128), BF16)
    r1 = iota16 + 1

    def twice(v):
        return jnp.concatenate([v, v], 0)

    def group(g, slot):
        base = pl.multiple_of(g * 8, 8)
        at = pl.ds(base, 8)
        for k, v in enumerate(spline(af_ref[at, :]) + spline(df_ref[at, :])):
            weights[slot, k] = v
        for i in range(8):
            def row(ref):
                return ref[pl.ds(base + i, 8, stride=0), :]

            def weight(k):
                return weights[slot, k, pl.ds(i, 8, stride=0), :]

            delta = iota8 - row(dur_ref)
            w = jnp.where(delta == 0, weight(4), 0.0)
            for k in range(1, 4):
                w = jnp.where(delta == k, weight(4 + k), w)
            e16 = twice(w * row(ex_ref)).astype(BF16)
            c16 = twice(w * row(cl_ref)).astype(BF16)
            code = twice(row(code_ref)).astype(F32).astype(BF16) - half16
            left_e, left_c = [], []
            for j in range(8):
                m = code == jnp.bfloat16(2 * j)
                left_e.append(jnp.where(m, e16, zero16))
                left_c.append(jnp.where(m, c16, zero16))
            left = jnp.concatenate(left_e + left_c, 0)
            age = twice(row(age_ref))
            kk = (r1 - age) & 15
            a = jnp.where(kk == 0, twice(weight(0)), 0.0)
            for k in range(1, 4):
                a = jnp.where(kk == k, twice(weight(k)), a)
            a16 = a.astype(BF16)
            block = ((age - 1 + kk) >> 4).astype(F32).astype(BF16)
            right = jnp.concatenate([jnp.where(block == jnp.bfloat16(q), a16, zero16) for q in range(8)], 0)
            res = lax.dot_general(left, right, (((1,), (1,)), ((), ())), preferred_element_type=F32)
            tile = tile_ref[g * 8 + i]
            acc[(tile & 1) * 32 + (tile >> 1)] += res

    def groups(step, carry):
        for slot in range(8):
            group(step * 8 + slot, slot)
        return carry

    def quarter(part, carry):
        for load in loads(part):
            load.wait()
        return lax.fori_loop(part * 2, part * 2 + 2, groups, carry)

    lax.fori_loop(0, 4, quarter, 0)

    low = iota8 < 4
    stores = []

    def joined(m, h, s):
        r8 = pl.multiple_of(lax.rem(m, 8) * 8, 8)
        up = jnp.minimum(m + 1, 31)
        dn = jnp.maximum(m - 1, 0)
        end = (iota8 == 0) & (m == 31)
        begin = (iota8 >= 5) & (m == 0)
        pooled = []
        for ch in range(2):
            total = jnp.zeros((8, 128), F32)
            for t in range(16):
                sl = pl.ds((ch * 16 + t) * 8, 8)
                ev = jnp.where(iota8 == 0, acc[up, sl, :], acc[m, sl, :])
                ev = pltpu.roll(jnp.where(end, 0.0, ev), 7, 0)
                od = jnp.where(iota8 >= 5, acc[32 + dn, sl, :], acc[32 + m, sl, :])
                v = ev + pltpu.roll(jnp.where(begin, 0.0, od), 3, 0)
                total = total + v
                z, y = t >> 1, 2 * (t & 1) + s
                out_ref[h, y * 8 + z if h == 0 else z * 4 + y, pl.ds(ch * 64 + r8, 8), :] = v
            pooled.append(total)
        pe, po = pooled
        at = lax.rem(m, 4) * 8 + m // 4
        pool_ref[0, at] = jnp.where(low, pe, pltpu.roll(po, 4, 0))
        pool_ref[1, at] = jnp.where(low, pltpu.roll(pe, 4, 0), po)

    for h in range(2):
        for s in range(2):
            first = h * 16 + s * 8

            def some(step, carry):
                for k in range(4):
                    joined(first + step * 4 + k, h, s)
                return carry

            lax.fori_loop(0, 2, some, 0)
            if h == 0:
                slots = [pl.ds(y * 8, 8) for y in (s, s + 2)]
            else:
                slots = [z * 4 + y for z in range(8) for y in (s, s + 2)]
            for k, at in enumerate(slots):
                stores.append(pltpu.make_async_copy(out_ref.at[h, at], out_hbm.at[h, at], out_sem.at[h * 2 + s, k]))
                stores[-1].start()
    stores.append(pltpu.make_async_copy(pool_ref, pool_hbm, out_sem.at[4, 0]))
    stores[-1].start()
    for store in stores:
        store.wait()


def grids(tiles, fields):
    whole = pl.BlockSpec(memory_space=HBM)
    return pl.pallas_call(
        grid_kernel,
        out_shape=(
            jax.ShapeDtypeStruct((2, 32, 128, 128), F32),
            jax.ShapeDtypeStruct((2, 32, 8, 128), F32),
        ),
        in_specs=[pl.BlockSpec(memory_space=pltpu.SMEM)] + [whole] * 7,
        out_specs=(whole, whole),
        scratch_shapes=[pltpu.VMEM((64, 256, 128), F32)]
        + [pltpu.VMEM((512, 128), I32)] * 3
        + [pltpu.VMEM((512, 128), F32)] * 4
        + [
            pltpu.VMEM((8, 8, 8, 128), F32),
            pltpu.VMEM((2, 32, 128, 128), F32),
            pltpu.VMEM((2, 32, 8, 128), F32),
            pltpu.SemaphoreType.DMA((4, 7)),
            pltpu.SemaphoreType.DMA((5, 16)),
        ],
        compiler_params=pltpu.CompilerParams(vmem_limit_bytes=63 << 20),
        cost_estimate=pl.CostEstimate(flops=2 * 512 * 256 * 128 * 128, bytes_accessed=6 << 20, transcendentals=0),
        name="local_grid",
    )(tiles, *fields)


def penalty(v, axis):
    n = v.shape[axis]
    place = lax.broadcasted_iota(I32, v.shape, axis)
    u = v - 2.0 * pltpu.roll(v, n - 1, axis) + pltpu.roll(v, n - 2, axis)
    u = jnp.where(place < n - 2, u, 0.0)
    return u - 2.0 * pltpu.roll(u, 1, axis) + pltpu.roll(u, 2, axis)


def chain_order(n):
    order = [(n // 2, 0)]
    for k in range(n // 2 - 1, 0, -1):
        order += [(k, 1), (k, 0)]
    return order


def reduce_along(n, me, neighbour, piece, land, send_sem, recv_sem, prepare, hook):
    order = chain_order(n)
    started = []

    def half_of(way, j):
        return order[j][1] if way == 0 else 1 - order[j][1]

    def transfer(way, j):
        k, _ = order[j]
        sub = half_of(way, j)
        dest = lax.rem(me + (k if way == 0 else n - k), n)
        return pltpu.make_async_remote_copy(
            src_ref=piece(dest, sub),
            dst_ref=land(way, j),
            send_sem=send_sem.at[way, j],
            recv_sem=recv_sem.at[way, j],
            device_id=neighbour(1 if way == 0 else n - 1),
            device_id_type=MESH,
        )

    def take(way, j, dest):
        transfer(way, j).wait_recv()
        target = piece(dest, half_of(way, j))
        target[...] += land(way, j)[...]

    for j, (k, first) in enumerate(order):
        for way in (0, 1):
            prepare(k, way)
            if (k + 1, first) in order:
                take(way, order.index((k + 1, first)), lax.rem(me + (k if way == 0 else n - k), n))
            move = transfer(way, j)
            move.start()
            started.append(move)
        hook(j)
    prepare(0, 0)
    for first in (1, 0):
        for way in (0, 1):
            take(way, order.index((1, first)), me)
    return started


def smooth_kernel(
    g_ref, p_ref, age_weight, dur_weight, credibility, out_s, out_r,
    part, other, land1, land2, grid, pool_in, pool_part, pool_y, pool_z, pool_zin, pool, twin, prior, field, done, got,
    local_sem, s0_send, s0_recv, s1_send, s1_recv, s2_send, s2_recv, ag_send, ag_recv,
    pa_send, pa_recv, pb_send, pb_recv, pc_send, pc_recv, x_send, x_recv, t_send, t_recv,
    y_send, y_recv, z_send, z_recv, o_send, o_recv,
):
    x, z, y, c = (lax.axis_index(a) for a in ("tg", "z", "y", "c"))
    sibling = (x, z, y, 1 - c)
    side = lax.rem(y, 2)
    pair = y + 1 - 2 * side

    def along_y(d):
        return (x, z, lax.rem(y + d, 4), c)

    def along_z(d):
        return (x, lax.rem(z + d, 8), y, c)

    def along_x(d):
        return (lax.rem(x + d, 4), z, y, c)

    barrier = pltpu.get_barrier_semaphore()
    peers = [sibling, (x, z, pair, 1 - c)]
    peers += [along_y(d) for d in range(1, 4)] + [along_z(d) for d in range(1, 8)] + [along_x(d) for d in range(1, 4)]
    for peer in peers:
        pl.semaphore_signal(barrier, inc=1, device_id=peer, device_id_type=MESH)
    pl.semaphore_wait(barrier, len(peers))

    def dests(n, i):
        order = [lax.rem(i + n // 2, n)]
        for k in range(n // 2 - 1, 0, -1):
            order += [lax.rem(i + k, n), lax.rem(i + n - k, n)]
        return order + [i]

    def arrive(dst, sem):
        pltpu.make_async_remote_copy(
            src_ref=dst, dst_ref=dst, send_sem=sem, recv_sem=sem, device_id=sibling, device_id_type=MESH
        ).wait_recv()

    def role(core, n, i, first_axis, n2, i2, second_axis, points):
        many = 32 // n
        half = many // 2
        sends = []

        def send(src, dst, s, r, peer):
            move = pltpu.make_async_remote_copy(
                src_ref=src, dst_ref=dst, send_sem=s, recv_sem=r, device_id=peer, device_id_type=MESH
            )
            move.start()
            sends.append(move)

        def pool_to_sibling():
            send(p_ref.at[1 - core], pool_in, pa_send.at[0], pa_recv.at[0], sibling)
            own = pltpu.make_async_copy(p_ref.at[core], pool_part, local_sem.at[8])
            own.start()
            return own

        def pool_along_y():
            pool_own.wait()
            arrive(pool_in, pa_recv.at[0])
            pool_part[...] += pool_in[...]
            for d in (2, 1, 3):
                at = pl.ds(lax.rem(y + d, 4) * 8, 8)
                send(pool_part.at[at], pool_y.at[d], pb_send.at[d], pb_recv.at[d], along_y(d))

        def pool_along_z():
            for d in range(1, 4):
                arrive(pool_y.at[d], pb_recv.at[d])
            pool_z[...] = (pool_part[pl.ds(y * 8, 8)] + pool_y[1]) + (pool_y[2] + pool_y[3])
            for d in (4, 3, 5, 2, 6, 1, 7):
                send(pool_z.at[lax.rem(z + d, 8)], pool_zin.at[d], pc_send.at[d], pc_recv.at[d], along_z(d))

        def pool_along_x():
            for d in range(1, 8):
                arrive(pool_zin.at[d], pc_recv.at[d])
            total = pool_z[z]
            for d in range(1, 8):
                total = total + pool_zin[d]
            pool[0] = total
            for d in (2, 1, 3):
                send(pool.at[0], pool.at[d], x_send.at[d], x_recv.at[d], along_x(d))

        def prior_to_sibling():
            for d in range(1, 4):
                arrive(pool.at[d], x_recv.at[d])
            total = (pool[0] + pool[1]) + (pool[2] + pool[3])
            twin[0] = pltpu.roll(total, 4, 0) / (1.0 + total)
            send(twin.at[0], twin.at[1], t_send.at[0], t_recv.at[0], sibling)

        def prior_along_y():
            arrive(twin.at[1], t_recv.at[0])
            low, high = twin[core], twin[1 - core]
            under = lax.broadcasted_iota(I32, (8, 128), 0) < 4
            prior[z, y] = jnp.where(under, low, pltpu.roll(high, 4, 0))
            for d in (2, 1, 3):
                send(prior.at[z, y], prior.at[z, y], y_send.at[d], y_recv.at[d], along_y(d))

        def prior_along_z():
            for d in range(1, 4):
                arrive(prior.at[z, lax.rem(y + 4 - d, 4)], y_recv.at[d])
            for d in (4, 3, 5, 2, 6, 1, 7):
                send(prior.at[z], prior.at[z], z_send.at[d], z_recv.at[d], along_z(d))

        pool_own = pool_to_sibling()
        sib_n, sib_i = (8, z) if core == 0 else (4, y)
        sib_many = 32 // sib_n
        for j, d in enumerate(dests(sib_n, sib_i)):
            at = pl.ds(d * sib_many, sib_many)
            send(g_ref.at[1 - core, at], other.at[at], s0_send.at[j], s0_recv.at[j], sibling)
        mine = []
        for j, d in enumerate(dests(n, i)):
            at = pl.ds(d * many, many)
            load = pltpu.make_async_copy(g_ref.at[core, at], part.at[at], local_sem.at[j])
            load.start()
            mine.append((load, at))
        ready = set()

        def prepare(k, way):
            j = 0 if k == n // 2 else (n - 1 if k == 0 else 1 + 2 * (n // 2 - 1 - k) + way)
            if j in ready:
                return
            ready.add(j)
            load, at = mine[j]
            load.wait()
            arrive(other.at[at], s0_recv.at[j])
            part[at] += other[at]

        def piece(d, sub):
            return part.at[pl.ds(d * many + sub * half, half)]

        def land(way, j):
            return land1.at[pl.ds((way * (n - 1) + j) * half, half)]

        def hook(j):
            if j in points:
                points[j](pool_along_z, pool_along_x, prior_to_sibling)

        pool_along_y()
        sends += reduce_along(n, i, first_axis, piece, land, s1_send, s1_recv, prepare, hook)

        far = sorted(range(1, n2), key=lambda d: -min(d, n2 - d))
        for d in far:
            send(part.at[i * many + lax.rem(i2 + d, n2)], land2.at[d], s2_send.at[d], s2_recv.at[d], second_axis(d))
        prior_along_y()
        quarter = 2 * core + side
        grid[quarter] = part[i * many + i2]
        for d in reversed(far):
            arrive(land2.at[d], s2_recv.at[d])
            grid[quarter] += land2[d]
        for j, peer in enumerate((sibling, (x, z, pair, c), (x, z, pair, 1 - c))):
            send(grid.at[quarter], grid.at[quarter], ag_send.at[j], ag_recv.at[j], peer)
        prior_along_z()
        for d in range(1, 8):
            arrive(prior.at[lax.rem(z + 8 - d, 8)], z_recv.at[d])
        for j, q in enumerate((2 * (1 - core) + side, 2 * core + 1 - side, 2 * (1 - core) + 1 - side)):
            arrive(grid.at[q], ag_recv.at[j])
        for move in sends:
            move.wait_send()

    def nth(k):
        return lambda *steps: steps[k]()

    @pl.when(c == 0)
    def _():
        role(0, 4, y, along_y, 8, z, along_z, {0: nth(0), 1: nth(1), 2: nth(2)})

    @pl.when(c == 1)
    def _():
        role(1, 8, z, along_z, 4, y, along_y, {1: nth(0), 3: nth(1), 5: nth(2)})

    quarter = 2 * c + side
    t = 2 * z + y // 2
    wa, wd, cred = age_weight[t], dur_weight[t], credibility[t]
    expo = jnp.concatenate([grid[q, 0:64] for q in range(4)], 0)
    claim = jnp.concatenate([grid[q, 64:128] for q in range(4)], 0)
    diagonal = expo + cred
    residual = claim + cred * prior[...].reshape(256, 128)
    direction = residual
    smoothed = jnp.zeros_like(residual)

    def dot(a, b):
        return jnp.sum(a * b, axis=(0, 1), keepdims=True)

    norm = dot(residual, residual)
    for _ in range(ITERS):
        image = diagonal * direction + wa * penalty(direction, 1) + wd * penalty(direction, 0)
        alpha = norm / dot(direction, image)
        smoothed = smoothed + alpha * direction
        residual = residual - alpha * image
        new = dot(residual, residual)
        direction = residual + (new / norm) * direction
        norm = new
    field[0] = smoothed
    field[1] = residual

    for j in range(8):
        at = pl.ds(pl.multiple_of(quarter * 64 + j * 8, 8), 8)
        for k in range(2):
            v = field[k, at]
            done[2 * j, k] = v[0:4]
            done[2 * j + 1, k] = v[4:8]

    chip = z * 4 + y

    def result(j):
        m = quarter * 8 + j // 2
        return jnp.logical_not((m == chip) & (j % 2 == c)), pltpu.make_async_remote_copy(
            src_ref=done.at[j], dst_ref=got.at[t], send_sem=o_send.at[j], recv_sem=o_recv.at[t],
            device_id=(x, quarter * 2 + j // 8, (j // 2) % 4, j % 2), device_id_type=MESH,
        )

    for j in range(16):
        away, move = result(j)
        pl.when(away)(move.start)
    here = z // 2 == quarter

    @pl.when(here)
    def _():
        got[t] = done[lax.rem(chip, 8) * 2 + c]

    for tt in range(16):
        @pl.when(jnp.logical_not(here & (t == tt)))
        def _():
            arrive(got.at[tt], o_recv.at[tt])

    out_s[...] = got[:, 0]
    out_r[...] = got[:, 1]
    for j in range(16):
        away, move = result(j)
        pl.when(away)(move.wait_send)


def smooth(parts, pooled, smooth_age, smooth_dur, credibility):
    smem = pl.BlockSpec(memory_space=pltpu.SMEM)
    vmem = pl.BlockSpec(memory_space=pltpu.VMEM)
    whole = pl.BlockSpec(memory_space=pl.ANY)
    dma = pltpu.SemaphoreType.DMA
    return pl.pallas_call(
        smooth_kernel,
        out_shape=(jax.ShapeDtypeStruct((16, 4, 128), F32),) * 2,
        in_specs=[whole, whole, smem, smem, smem],
        out_specs=(vmem, vmem),
        scratch_shapes=[
            pltpu.VMEM((32, 128, 128), F32),
            pltpu.VMEM((32, 128, 128), F32),
            pltpu.VMEM((28, 128, 128), F32),
            pltpu.VMEM((8, 128, 128), F32),
            pltpu.VMEM((4, 128, 128), F32),
            pltpu.VMEM((32, 8, 128), F32),
            pltpu.VMEM((32, 8, 128), F32),
            pltpu.VMEM((4, 8, 8, 128), F32),
            pltpu.VMEM((8, 8, 128), F32),
            pltpu.VMEM((8, 8, 128), F32),
            pltpu.VMEM((4, 8, 128), F32),
            pltpu.VMEM((2, 8, 128), F32),
            pltpu.VMEM((8, 4, 8, 128), F32),
            pltpu.VMEM((2, 256, 128), F32),
            pltpu.VMEM((16, 2, 4, 128), F32),
            pltpu.VMEM((16, 2, 4, 128), F32),
            dma((9,)), dma((8,)), dma((8,)),
            dma((2, 7)), dma((2, 7)), dma((8,)), dma((8,)), dma((3,)), dma((3,)),
            dma((1,)), dma((1,)), dma((4,)), dma((4,)), dma((8,)), dma((8,)),
            dma((4,)), dma((4,)), dma((1,)), dma((1,)),
            dma((4,)), dma((4,)), dma((8,)), dma((8,)), dma((16,)), dma((16,)),
        ],
        compiler_params=pltpu.CompilerParams(collective_id=0, has_side_effects=True, vmem_limit_bytes=63 << 20),
        cost_estimate=pl.CostEstimate(flops=20 << 20, bytes_accessed=6 << 20, transcendentals=0),
        name="reduce_and_smooth",
    )(parts, pooled, smooth_age, smooth_dur, credibility)


def per_device(
    age_cell, dur_cell, trans_code, age_frac, dur_frac, exposure, claims, block_tile, smooth_age, smooth_dur, credibility
):
    fields = [
        f.reshape(-1, 128) for f in (age_cell, dur_cell, trans_code, age_frac, dur_frac, exposure, claims)
    ]
    parts, pooled = grids(block_tile.reshape(-1), fields)
    return smooth(parts, pooled, smooth_age, smooth_dur, credibility)


def solution(mesh):
    split = Mesh(mesh.devices.reshape(mesh.shape["tg"], 8, 4, 2), ("tg", "z", "y", "c"))
    tile = ("z", "y", "c")
    placed = (P("tg", tile),) * 7 + (P("tg", tile, None),) + (P("tg"),) * 3
    return jax.shard_map(
        per_device,
        mesh=split,
        in_specs=placed,
        out_specs=(P("tg", tile, None),) * 2,
        check_vma=False,
    )
```

```python
import jax, jax.numpy as jnp
from jax import lax
from jax.experimental import pallas as pl
from jax.experimental.pallas import tpu as pltpu
from jax.sharding import Mesh
from jax.sharding import PartitionSpec as P

ITERS = 4
MESH = pl.DeviceIdType.MESH
HBM = pltpu.MemorySpace.HBM
F32, BF16, I32 = jnp.float32, jnp.bfloat16, jnp.int32

def spline(f):
    r = 1.0 - f
    f2 = f * f
    c = f2 * f
    s = 1.0 / 6.0
    return (r * r * r * s, (3.0 * c - 6.0 * f2 + 4.0) * s, (-3.0 * c + 3.0 * f2 + 3.0 * f + 1.0) * s, c * s)

def grid_kernel(
    tile_ref, age_hbm, dur_hbm, code_hbm, af_hbm, df_hbm, ex_hbm, cl_hbm, out_hbm, pool_hbm,
    acc, age_ref, dur_ref, code_ref, af_ref, df_ref, ex_ref, cl_ref, weights, out_ref, pool_ref, sem, out_sem,
):
    pairs = (
        (age_hbm, age_ref), (dur_hbm, dur_ref), (code_hbm, code_ref), (af_hbm, af_ref),
        (df_hbm, df_ref), (ex_hbm, ex_ref), (cl_hbm, cl_ref),
    )

    def loads(part):
        at = pl.ds(part * 128, 128)
        return [pltpu.make_async_copy(src.at[at], dst.at[at], sem.at[part, k]) for k, (src, dst) in enumerate(pairs)]

    for part in range(4):
        for load in loads(part):
            load.start()
    acc[...] = jnp.zeros(acc.shape, F32)
    iota8 = lax.broadcasted_iota(I32, (8, 128), 0)
    iota16 = lax.broadcasted_iota(I32, (16, 128), 0)
    half16 = (iota16 >> 3).astype(F32).astype(BF16)
    zero16 = jnp.zeros((16, 128), BF16)
    r1 = iota16 + 1

    def twice(v):
        return jnp.concatenate([v, v], 0)

    def group(g, slot):
        base = pl.multiple_of(g * 8, 8)
        at = pl.ds(base, 8)
        for k, v in enumerate(spline(af_ref[at, :]) + spline(df_ref[at, :])):
            weights[slot, k] = v
        for i in range(8):
            def row(ref):
                return ref[pl.ds(base + i, 8, stride=0), :]

            def weight(k):
                return weights[slot, k, pl.ds(i, 8, stride=0), :]

            delta = iota8 - row(dur_ref)
            w = jnp.where(delta == 0, weight(4), 0.0)
            for k in range(1, 4):
                w = jnp.where(delta == k, weight(4 + k), w)
            e16 = twice(w * row(ex_ref)).astype(BF16)
            c16 = twice(w * row(cl_ref)).astype(BF16)
            code = twice(row(code_ref)).astype(F32).astype(BF16) - half16
            left_e, left_c = [], []
            for j in range(8):
                m = code == jnp.bfloat16(2 * j)
                left_e.append(jnp.where(m, e16, zero16))
                left_c.append(jnp.where(m, c16, zero16))
            left = jnp.concatenate(left_e + left_c, 0)
            age = twice(row(age_ref))
            kk = (r1 - age) & 15
            a = jnp.where(kk == 0, twice(weight(0)), 0.0)
            for k in range(1, 4):
                a = jnp.where(kk == k, twice(weight(k)), a)
            a16 = a.astype(BF16)
            block = ((age - 1 + kk) >> 4).astype(F32).astype(BF16)
            right = jnp.concatenate([jnp.where(block == jnp.bfloat16(q), a16, zero16) for q in range(8)], 0)
            res = lax.dot_general(left, right, (((1,), (1,)), ((), ())), preferred_element_type=F32)
            tile = tile_ref[g * 8 + i]
            acc[(tile & 1) * 32 + (tile >> 1)] += res

    def groups(step, carry):
        for slot in range(8):
            group(step * 8 + slot, slot)
        return carry

    def quarter(part, carry):
        for load in loads(part):
            load.wait()
        return lax.fori_loop(part * 2, part * 2 + 2, groups, carry)

    lax.fori_loop(0, 4, quarter, 0)

    low = iota8 < 4
    stores = []

    def joined(m, h, s):
        r8 = pl.multiple_of(lax.rem(m, 8) * 8, 8)
        up = jnp.minimum(m + 1, 31)
        dn = jnp.maximum(m - 1, 0)
        end = (iota8 == 0) & (m == 31)
        begin = (iota8 >= 5) & (m == 0)
        pooled = []
        for ch in range(2):
            total = jnp.zeros((8, 128), F32)
            for t in range(16):
                sl = pl.ds((ch * 16 + t) * 8, 8)
                ev = jnp.where(iota8 == 0, acc[up, sl, :], acc[m, sl, :])
                ev = pltpu.roll(jnp.where(end, 0.0, ev), 7, 0)
                od = jnp.where(iota8 >= 5, acc[32 + dn, sl, :], acc[32 + m, sl, :])
                v = ev + pltpu.roll(jnp.where(begin, 0.0, od), 3, 0)
                total = total + v
                z, y = t >> 1, 2 * (t & 1) + s
                out_ref[h, y * 8 + z if h == 0 else z * 4 + y, pl.ds(ch * 64 + r8, 8), :] = v
            pooled.append(total)
        pe, po = pooled
        at = lax.rem(m, 4) * 8 + m // 4
        pool_ref[0, at] = jnp.where(low, pe, pltpu.roll(po, 4, 0))
        pool_ref[1, at] = jnp.where(low, pltpu.roll(pe, 4, 0), po)

    for h in range(2):
        for s in range(2):
            first = h * 16 + s * 8

            def some(step, carry):
                for k in range(4):
                    joined(first + step * 4 + k, h, s)
                return carry

            lax.fori_loop(0, 2, some, 0)
            if h == 0:
                slots = [pl.ds(y * 8, 8) for y in (s, s + 2)]
            else:
                slots = [z * 4 + y for z in range(8) for y in (s, s + 2)]
            for k, at in enumerate(slots):
                stores.append(pltpu.make_async_copy(out_ref.at[h, at], out_hbm.at[h, at], out_sem.at[h * 2 + s, k]))
                stores[-1].start()
    stores.append(pltpu.make_async_copy(pool_ref, pool_hbm, out_sem.at[4, 0]))
    stores[-1].start()
    for store in stores:
        store.wait()


def grids(tiles, fields):
    whole = pl.BlockSpec(memory_space=HBM)
    return pl.pallas_call(
        grid_kernel,
        out_shape=(
            jax.ShapeDtypeStruct((2, 32, 128, 128), F32),
            jax.ShapeDtypeStruct((2, 32, 8, 128), F32),
        ),
        in_specs=[pl.BlockSpec(memory_space=pltpu.SMEM)] + [whole] * 7,
        out_specs=(whole, whole),
        scratch_shapes=[pltpu.VMEM((64, 256, 128), F32)]
        + [pltpu.VMEM((512, 128), I32)] * 3
        + [pltpu.VMEM((512, 128), F32)] * 4
        + [
            pltpu.VMEM((8, 8, 8, 128), F32),
            pltpu.VMEM((2, 32, 128, 128), F32),
            pltpu.VMEM((2, 32, 8, 128), F32),
            pltpu.SemaphoreType.DMA((4, 7)),
            pltpu.SemaphoreType.DMA((5, 16)),
        ],
        compiler_params=pltpu.CompilerParams(vmem_limit_bytes=63 << 20),
        cost_estimate=pl.CostEstimate(flops=2 * 512 * 256 * 128 * 128, bytes_accessed=6 << 20, transcendentals=0),
        name="local_grid",
    )(tiles, *fields)


def penalty(v, axis):
    n = v.shape[axis]
    place = lax.broadcasted_iota(I32, v.shape, axis)
    u = v - 2.0 * pltpu.roll(v, n - 1, axis) + pltpu.roll(v, n - 2, axis)
    u = jnp.where(place < n - 2, u, 0.0)
    return u - 2.0 * pltpu.roll(u, 1, axis) + pltpu.roll(u, 2, axis)


def chain_order(n):
    order = [(n // 2, 0)]
    for k in range(n // 2 - 1, 0, -1):
        order += [(k, 1), (k, 0)]
    return order


def reduce_along(n, me, neighbour, piece, land, send_sem, recv_sem, prepare, hook):
    order = chain_order(n)
    started = []

    def half_of(way, j):
        return order[j][1] if way == 0 else 1 - order[j][1]

    def transfer(way, j):
        k, _ = order[j]
        sub = half_of(way, j)
        dest = lax.rem(me + (k if way == 0 else n - k), n)
        return pltpu.make_async_remote_copy(
            src_ref=piece(dest, sub),
            dst_ref=land(way, j),
            send_sem=send_sem.at[way, j],
            recv_sem=recv_sem.at[way, j],
            device_id=neighbour(1 if way == 0 else n - 1),
            device_id_type=MESH,
        )

    def take(way, j, dest):
        transfer(way, j).wait_recv()
        target = piece(dest, half_of(way, j))
        target[...] += land(way, j)[...]

    for j, (k, first) in enumerate(order):
        for way in (0, 1):
            prepare(k, way)
            if (k + 1, first) in order:
                take(way, order.index((k + 1, first)), lax.rem(me + (k if way == 0 else n - k), n))
            move = transfer(way, j)
            move.start()
            started.append(move)
        hook(j)
    prepare(0, 0)
    for first in (1, 0):
        for way in (0, 1):
            take(way, order.index((1, first)), me)
    return started


def smooth_kernel(
    g_ref, p_ref, age_weight, dur_weight, credibility, out_s, out_r,
    part, other, land1, land2, grid, pool_y, pool_z, pool_zin, pool, prior, field, done, got,
    local_sem, s0_send, s0_recv, s1_send, s1_recv, s2_send, s2_recv, ag_send, ag_recv,
    pb_send, pb_recv, pc_send, pc_recv, x_send, x_recv, y_send, y_recv, z_send, z_recv, o_send, o_recv,
):
    x, z, y, c = (lax.axis_index(a) for a in ("tg", "z", "y", "c"))
    sibling = (x, z, y, 1 - c)
    side = lax.rem(y, 2)
    pair = y + 1 - 2 * side

    def along_y(d):
        return (x, z, lax.rem(y + d, 4), c)

    def along_z(d):
        return (x, lax.rem(z + d, 8), y, c)

    barrier = pltpu.get_barrier_semaphore()
    peers = [sibling] + [along_z(d) for d in range(1, 8)]
    for e in (c, 1 - c):
        peers += [(x, z, lax.rem(y + d, 4), e) for d in range(1, 4)] + [(lax.rem(x + d, 4), z, y, e) for d in range(1, 4)]
    for peer in peers:
        pl.semaphore_signal(barrier, inc=1, device_id=peer, device_id_type=MESH)
    pl.semaphore_wait(barrier, len(peers))

    def dests(n, i):
        order = [lax.rem(i + n // 2, n)]
        for k in range(n // 2 - 1, 0, -1):
            order += [lax.rem(i + k, n), lax.rem(i + n - k, n)]
        return order + [i]

    def arrive(dst, sem):
        pltpu.make_async_remote_copy(
            src_ref=dst, dst_ref=dst, send_sem=sem, recv_sem=sem, device_id=sibling, device_id_type=MESH
        ).wait_recv()

    def role(core, n, i, first_axis, n2, i2, second_axis, points):
        many = 32 // n
        half = many // 2
        sends = []

        def send(src, dst, s, r, peer):
            move = pltpu.make_async_remote_copy(
                src_ref=src, dst_ref=dst, send_sem=s, recv_sem=r, device_id=peer, device_id_type=MESH
            )
            move.start()
            sends.append(move)

        def pool_along_y():
            own = pltpu.make_async_copy(p_ref.at[core, pl.ds(y * 8, 8)], pool_y.at[0], local_sem.at[8])
            own.start()
            for k in (4, 5, 2, 3, 6, 7, 1):
                d, e = k // 2, k % 2
                to, yy = core ^ e, lax.rem(y + d, 4)
                send(p_ref.at[to, pl.ds(yy * 8, 8)], pool_y.at[k], pb_send.at[k], pb_recv.at[k], (x, z, yy, to))
            return own

        def pool_along_z():
            pool_own.wait()
            total = pool_y[0]
            for k in range(1, 8):
                arrive(pool_y.at[k], pb_recv.at[k])
                total = total + pool_y[k]
            pool_z[...] = total
            for d in (4, 3, 5, 2, 6, 1, 7):
                send(pool_z.at[lax.rem(z + d, 8)], pool_zin.at[d], pc_send.at[d], pc_recv.at[d], along_z(d))

        def pool_along_x():
            total = pool_z[z]
            for d in range(1, 8):
                arrive(pool_zin.at[d], pc_recv.at[d])
                total = total + pool_zin[d]
            pool[0] = total
            for d in (2, 1, 3):
                send(pool.at[0], pool.at[d], x_send.at[d], x_recv.at[d], (lax.rem(x + d, 4), z, y, core))

        def prior_along_z():
            for d in range(1, 4):
                arrive(pool.at[d], x_recv.at[d])
            total = (pool[0] + pool[1]) + (pool[2] + pool[3])
            prior[y * 2 + core, z] = pltpu.roll(total, 4, 0) / (1.0 + total)
            for d in (4, 3, 5, 2, 6, 1, 7):
                at = prior.at[y * 2 + core, z]
                send(at, at, z_send.at[d], z_recv.at[d], along_z(d))

        def prior_along_y():
            for d in range(1, 8):
                arrive(prior.at[y * 2 + core, lax.rem(z + 8 - d, 8)], z_recv.at[d])
            for k in (4, 5, 2, 3, 6, 7, 1):
                at = prior.at[y * 2 + core]
                send(at, at, y_send.at[k], y_recv.at[k], (x, z, lax.rem(y + k // 2, 4), core ^ (k % 2)))

        pool_own = pool_along_y()
        sib_n, sib_i = (8, z) if core == 0 else (4, y)
        sib_many = 32 // sib_n
        for j, d in enumerate(dests(sib_n, sib_i)):
            at = pl.ds(d * sib_many, sib_many)
            send(g_ref.at[1 - core, at], other.at[at], s0_send.at[j], s0_recv.at[j], sibling)
        mine = []
        for j, d in enumerate(dests(n, i)):
            at = pl.ds(d * many, many)
            load = pltpu.make_async_copy(g_ref.at[core, at], part.at[at], local_sem.at[j])
            load.start()
            mine.append((load, at))
        ready = set()

        def prepare(k, way):
            j = 0 if k == n // 2 else (n - 1 if k == 0 else 1 + 2 * (n // 2 - 1 - k) + way)
            if j in ready:
                return
            ready.add(j)
            load, at = mine[j]
            load.wait()
            arrive(other.at[at], s0_recv.at[j])
            part[at] += other[at]

        def piece(d, sub):
            return part.at[pl.ds(d * many + sub * half, half)]

        def land(way, j):
            return land1.at[pl.ds((way * (n - 1) + j) * half, half)]

        def hook(j):
            if j in points:
                points[j](pool_along_z, pool_along_x, prior_along_z)

        sends += reduce_along(n, i, first_axis, piece, land, s1_send, s1_recv, prepare, hook)

        far = sorted(range(1, n2), key=lambda d: -min(d, n2 - d))
        for d in far:
            send(part.at[i * many + lax.rem(i2 + d, n2)], land2.at[d], s2_send.at[d], s2_recv.at[d], second_axis(d))
        prior_along_y()
        quarter = 2 * core + side
        grid[quarter] = part[i * many + i2]
        for d in reversed(far):
            arrive(land2.at[d], s2_recv.at[d])
            grid[quarter] += land2[d]
        for j, peer in enumerate((sibling, (x, z, pair, c), (x, z, pair, 1 - c))):
            send(grid.at[quarter], grid.at[quarter], ag_send.at[j], ag_recv.at[j], peer)
        for k in range(1, 8):
            arrive(prior.at[lax.rem(y + 4 - k // 2, 4) * 2 + (core ^ (k % 2))], y_recv.at[k])
        for j, q in enumerate((2 * (1 - core) + side, 2 * core + 1 - side, 2 * (1 - core) + 1 - side)):
            arrive(grid.at[q], ag_recv.at[j])
        for move in sends:
            move.wait_send()

    def nth(k):
        return lambda *steps: steps[k]()

    @pl.when(c == 0)
    def _():
        role(0, 4, y, along_y, 8, z, along_z, {0: nth(0), 1: nth(1), 2: nth(2)})

    @pl.when(c == 1)
    def _():
        role(1, 8, z, along_z, 4, y, along_y, {1: nth(0), 3: nth(1), 5: nth(2)})

    quarter = 2 * c + side
    t = 2 * z + y // 2
    wa, wd, cred = age_weight[t], dur_weight[t], credibility[t]
    expo = jnp.concatenate([grid[q, 0:64] for q in range(4)], 0)
    claim = jnp.concatenate([grid[q, 64:128] for q in range(4)], 0)
    diagonal = expo + cred
    under = lax.broadcasted_iota(I32, (8, 128), 0) < 4
    pooled = [
        jnp.where(under, prior[2 * yy, zz], pltpu.roll(prior[2 * yy + 1, zz], 4, 0)) for zz in range(8) for yy in range(4)
    ]
    residual = claim + cred * jnp.concatenate(pooled, 0)
    direction = residual
    smoothed = jnp.zeros_like(residual)

    def dot(a, b):
        return jnp.sum(a * b, axis=(0, 1), keepdims=True)

    norm = dot(residual, residual)
    for _ in range(ITERS):
        image = diagonal * direction + wa * penalty(direction, 1) + wd * penalty(direction, 0)
        alpha = norm / dot(direction, image)
        smoothed = smoothed + alpha * direction
        residual = residual - alpha * image
        new = dot(residual, residual)
        direction = residual + (new / norm) * direction
        norm = new
    field[0] = smoothed
    field[1] = residual

    for j in range(8):
        at = pl.ds(pl.multiple_of(quarter * 64 + j * 8, 8), 8)
        for k in range(2):
            v = field[k, at]
            done[2 * j, k] = v[0:4]
            done[2 * j + 1, k] = v[4:8]

    chip = z * 4 + y

    def result(j):
        m = quarter * 8 + j // 2
        return jnp.logical_not((m == chip) & (j % 2 == c)), pltpu.make_async_remote_copy(
            src_ref=done.at[j], dst_ref=got.at[t], send_sem=o_send.at[j], recv_sem=o_recv.at[t],
            device_id=(x, quarter * 2 + j // 8, (j // 2) % 4, j % 2), device_id_type=MESH,
        )

    for j in range(16):
        away, move = result(j)
        pl.when(away)(move.start)
    here = z // 2 == quarter

    @pl.when(here)
    def _():
        got[t] = done[lax.rem(chip, 8) * 2 + c]

    for tt in range(16):
        @pl.when(jnp.logical_not(here & (t == tt)))
        def _():
            arrive(got.at[tt], o_recv.at[tt])

    out_s[...] = got[:, 0]
    out_r[...] = got[:, 1]
    for j in range(16):
        away, move = result(j)
        pl.when(away)(move.wait_send)


def smooth(parts, pooled, smooth_age, smooth_dur, credibility):
    smem = pl.BlockSpec(memory_space=pltpu.SMEM)
    vmem = pl.BlockSpec(memory_space=pltpu.VMEM)
    whole = pl.BlockSpec(memory_space=pl.ANY)
    dma = pltpu.SemaphoreType.DMA
    return pl.pallas_call(
        smooth_kernel,
        out_shape=(jax.ShapeDtypeStruct((16, 4, 128), F32),) * 2,
        in_specs=[whole, whole, smem, smem, smem],
        out_specs=(vmem, vmem),
        scratch_shapes=[
            pltpu.VMEM((32, 128, 128), F32),
            pltpu.VMEM((32, 128, 128), F32),
            pltpu.VMEM((28, 128, 128), F32),
            pltpu.VMEM((8, 128, 128), F32),
            pltpu.VMEM((4, 128, 128), F32),
            pltpu.VMEM((8, 8, 8, 128), F32),
            pltpu.VMEM((8, 8, 128), F32),
            pltpu.VMEM((8, 8, 128), F32),
            pltpu.VMEM((8, 8, 128), F32),
            pltpu.VMEM((8, 8, 8, 128), F32),
            pltpu.VMEM((2, 256, 128), F32),
            pltpu.VMEM((16, 2, 4, 128), F32),
            pltpu.VMEM((16, 2, 4, 128), F32),
            dma((9,)), dma((8,)), dma((8,)),
            dma((2, 7)), dma((2, 7)), dma((8,)), dma((8,)), dma((3,)), dma((3,)),
            dma((8,)), dma((8,)), dma((8,)), dma((8,)), dma((8,)), dma((8,)),
            dma((8,)), dma((8,)), dma((8,)), dma((8,)), dma((16,)), dma((16,)),
        ],
        compiler_params=pltpu.CompilerParams(collective_id=0, has_side_effects=True, vmem_limit_bytes=(64 << 20) - (200 << 10)),
        cost_estimate=pl.CostEstimate(flops=20 << 20, bytes_accessed=6 << 20, transcendentals=0),
        name="reduce_and_smooth",
    )(parts, pooled, smooth_age, smooth_dur, credibility)


def per_device(
    age_cell, dur_cell, trans_code, age_frac, dur_frac, exposure, claims, block_tile, smooth_age, smooth_dur, credibility
):
    fields = [
        f.reshape(-1, 128) for f in (age_cell, dur_cell, trans_code, age_frac, dur_frac, exposure, claims)
    ]
    parts, pooled = grids(block_tile.reshape(-1), fields)
    return smooth(parts, pooled, smooth_age, smooth_dur, credibility)


def solution(mesh):
    split = Mesh(mesh.devices.reshape(mesh.shape["tg"], 8, 4, 2), ("tg", "z", "y", "c"))
    tile = ("z", "y", "c")
    placed = (P("tg", tile),) * 7 + (P("tg", tile, None),) + (P("tg"),) * 3
    return jax.shard_map(
        per_device,
        mesh=split,
        in_specs=placed,
        out_specs=(P("tg", tile, None),) * 2,
        check_vma=False,
    )
```

```python
import jax, jax.numpy as jnp
from jax import lax
from jax.experimental import pallas as pl
from jax.experimental.pallas import tpu as pltpu
from jax.sharding import Mesh
from jax.sharding import PartitionSpec as P

ITERS = 4
MESH = pl.DeviceIdType.MESH
HBM = pltpu.MemorySpace.HBM
F32, BF16, I32 = jnp.float32, jnp.bfloat16, jnp.int32

def spline(f):
    r = 1.0 - f
    f2 = f * f
    c = f2 * f
    s = 1.0 / 6.0
    return (r * r * r * s, (3.0 * c - 6.0 * f2 + 4.0) * s, (-3.0 * c + 3.0 * f2 + 3.0 * f + 1.0) * s, c * s)

def grid_kernel(
    tile_ref, age_hbm, dur_hbm, code_hbm, af_hbm, df_hbm, ex_hbm, cl_hbm, out_hbm, pool_hbm,
    acc, age_ref, dur_ref, code_ref, af_ref, df_ref, ex_ref, cl_ref, weights, out_ref, pool_ref, sem, out_sem,
):
    pairs = (
        (age_hbm, age_ref), (dur_hbm, dur_ref), (code_hbm, code_ref), (af_hbm, af_ref),
        (df_hbm, df_ref), (ex_hbm, ex_ref), (cl_hbm, cl_ref),
    )

    def loads(part):
        at = pl.ds(part * 128, 128)
        return [pltpu.make_async_copy(src.at[at], dst.at[at], sem.at[part, k]) for k, (src, dst) in enumerate(pairs)]

    for part in range(4):
        for load in loads(part):
            load.start()
    acc[...] = jnp.zeros(acc.shape, F32)
    iota8 = lax.broadcasted_iota(I32, (8, 128), 0)
    iota16 = lax.broadcasted_iota(I32, (16, 128), 0)
    half16 = (iota16 >> 3).astype(F32).astype(BF16)
    zero16 = jnp.zeros((16, 128), BF16)
    r1 = iota16 + 1

    def twice(v):
        return jnp.concatenate([v, v], 0)

    def group(g, slot):
        base = pl.multiple_of(g * 8, 8)
        at = pl.ds(base, 8)
        for k, v in enumerate(spline(af_ref[at, :]) + spline(df_ref[at, :])):
            weights[slot, k] = v
        for i in range(8):
            def row(ref):
                return ref[pl.ds(base + i, 8, stride=0), :]

            def weight(k):
                return weights[slot, k, pl.ds(i, 8, stride=0), :]

            delta = iota8 - row(dur_ref)
            w = jnp.where(delta == 0, weight(4), 0.0)
            for k in range(1, 4):
                w = jnp.where(delta == k, weight(4 + k), w)
            e16 = twice(w * row(ex_ref)).astype(BF16)
            c16 = twice(w * row(cl_ref)).astype(BF16)
            code = twice(row(code_ref)).astype(F32).astype(BF16) - half16
            left_e, left_c = [], []
            for j in range(8):
                m = code == jnp.bfloat16(2 * j)
                left_e.append(jnp.where(m, e16, zero16))
                left_c.append(jnp.where(m, c16, zero16))
            left = jnp.concatenate(left_e + left_c, 0)
            age = twice(row(age_ref))
            kk = (r1 - age) & 15
            a = jnp.where(kk == 0, twice(weight(0)), 0.0)
            for k in range(1, 4):
                a = jnp.where(kk == k, twice(weight(k)), a)
            a16 = a.astype(BF16)
            block = ((age - 1 + kk) >> 4).astype(F32).astype(BF16)
            right = jnp.concatenate([jnp.where(block == jnp.bfloat16(q), a16, zero16) for q in range(8)], 0)
            res = lax.dot_general(left, right, (((1,), (1,)), ((), ())), preferred_element_type=F32)
            tile = tile_ref[g * 8 + i]
            acc[(tile & 1) * 32 + (tile >> 1)] += res

    def groups(step, carry):
        for slot in range(8):
            group(step * 8 + slot, slot)
        return carry

    def quarter(part, carry):
        for load in loads(part):
            load.wait()
        return lax.fori_loop(part * 2, part * 2 + 2, groups, carry)

    lax.fori_loop(0, 4, quarter, 0)

    low = iota8 < 4
    stores = []

    def joined(m, h, s):
        r8 = pl.multiple_of(lax.rem(m, 8) * 8, 8)
        up = jnp.minimum(m + 1, 31)
        dn = jnp.maximum(m - 1, 0)
        end = (iota8 == 0) & (m == 31)
        begin = (iota8 >= 5) & (m == 0)
        pooled = []
        for ch in range(2):
            total = jnp.zeros((8, 128), F32)
            for t in range(16):
                sl = pl.ds((ch * 16 + t) * 8, 8)
                ev = jnp.where(iota8 == 0, acc[up, sl, :], acc[m, sl, :])
                ev = pltpu.roll(jnp.where(end, 0.0, ev), 7, 0)
                od = jnp.where(iota8 >= 5, acc[32 + dn, sl, :], acc[32 + m, sl, :])
                v = ev + pltpu.roll(jnp.where(begin, 0.0, od), 3, 0)
                total = total + v
                z, y = t >> 1, 2 * (t & 1) + s
                out_ref[h, y * 8 + z if h == 0 else z * 4 + y, pl.ds(ch * 64 + r8, 8), :] = v
            pooled.append(total)
        pe, po = pooled
        at = lax.rem(m, 4) * 8 + m // 4
        pool_ref[0, at] = jnp.where(low, pe, pltpu.roll(po, 4, 0))
        pool_ref[1, at] = jnp.where(low, pltpu.roll(pe, 4, 0), po)

    for h in range(2):
        for s in range(2):
            first = h * 16 + s * 8

            def some(step, carry):
                for k in range(4):
                    joined(first + step * 4 + k, h, s)
                return carry

            lax.fori_loop(0, 2, some, 0)
            if h == 0:
                slots = [pl.ds(y * 8, 8) for y in (s, s + 2)]
            else:
                slots = [z * 4 + y for z in range(8) for y in (s, s + 2)]
            for k, at in enumerate(slots):
                stores.append(pltpu.make_async_copy(out_ref.at[h, at], out_hbm.at[h, at], out_sem.at[h * 2 + s, k]))
                stores[-1].start()
    stores.append(pltpu.make_async_copy(pool_ref, pool_hbm, out_sem.at[4, 0]))
    stores[-1].start()
    for store in stores:
        store.wait()


def grids(tiles, fields):
    whole = pl.BlockSpec(memory_space=HBM)
    return pl.pallas_call(
        grid_kernel,
        out_shape=(
            jax.ShapeDtypeStruct((2, 32, 128, 128), F32),
            jax.ShapeDtypeStruct((2, 32, 8, 128), F32),
        ),
        in_specs=[pl.BlockSpec(memory_space=pltpu.SMEM)] + [whole] * 7,
        out_specs=(whole, whole),
        scratch_shapes=[pltpu.VMEM((64, 256, 128), F32)]
        + [pltpu.VMEM((512, 128), I32)] * 3
        + [pltpu.VMEM((512, 128), F32)] * 4
        + [
            pltpu.VMEM((8, 8, 8, 128), F32),
            pltpu.VMEM((2, 32, 128, 128), F32),
            pltpu.VMEM((2, 32, 8, 128), F32),
            pltpu.SemaphoreType.DMA((4, 7)),
            pltpu.SemaphoreType.DMA((5, 16)),
        ],
        compiler_params=pltpu.CompilerParams(vmem_limit_bytes=63 << 20),
        cost_estimate=pl.CostEstimate(flops=2 * 512 * 256 * 128 * 128, bytes_accessed=6 << 20, transcendentals=0),
        name="local_grid",
    )(tiles, *fields)


def penalty(v, axis):
    n = v.shape[axis]
    place = lax.broadcasted_iota(I32, v.shape, axis)
    u = v - 2.0 * pltpu.roll(v, n - 1, axis) + pltpu.roll(v, n - 2, axis)
    u = jnp.where(place < n - 2, u, 0.0)
    return u - 2.0 * pltpu.roll(u, 1, axis) + pltpu.roll(u, 2, axis)


def chain_order(n):
    order = [(n // 2, 0)]
    for k in range(n // 2 - 1, 0, -1):
        order += [(k, 1), (k, 0)]
    return order


def reduce_along(n, me, neighbour, piece, land, send_sem, recv_sem, prepare, hook):
    order = chain_order(n)
    started = []

    def half_of(way, j):
        return order[j][1] if way == 0 else 1 - order[j][1]

    def transfer(way, j):
        k, _ = order[j]
        sub = half_of(way, j)
        dest = lax.rem(me + (k if way == 0 else n - k), n)
        return pltpu.make_async_remote_copy(
            src_ref=piece(dest, sub),
            dst_ref=land(way, j),
            send_sem=send_sem.at[way, j],
            recv_sem=recv_sem.at[way, j],
            device_id=neighbour(1 if way == 0 else n - 1),
            device_id_type=MESH,
        )

    def take(way, j, dest):
        transfer(way, j).wait_recv()
        target = piece(dest, half_of(way, j))
        target[...] += land(way, j)[...]

    for j, (k, first) in enumerate(order):
        for way in (0, 1):
            prepare(k, way)
            if (k + 1, first) in order:
                take(way, order.index((k + 1, first)), lax.rem(me + (k if way == 0 else n - k), n))
            move = transfer(way, j)
            move.start()
            started.append(move)
        hook(j)
    prepare(0, 0)
    for first in (1, 0):
        for way in (0, 1):
            take(way, order.index((1, first)), me)
    return started


def smooth_kernel(
    g_ref, p_ref, age_weight, dur_weight, credibility, out_s, out_r,
    part, other, land1, land2, grid, pool_y, pool_z, pool_zin, pool, prior, field, done, got,
    local_sem, s0_send, s0_recv, s1_send, s1_recv, s2_send, s2_recv, ag_send, ag_recv,
    pb_send, pb_recv, pc_send, pc_recv, x_send, x_recv, y_send, y_recv, z_send, z_recv, o_send, o_recv,
):
    x, z, y, c = (lax.axis_index(a) for a in ("tg", "z", "y", "c"))
    sibling = (x, z, y, 1 - c)
    side = lax.rem(y, 2)
    pair = y + 1 - 2 * side

    def along_y(d):
        return (x, z, lax.rem(y + d, 4), c)

    def along_z(d):
        return (x, lax.rem(z + d, 8), y, c)

    barrier = pltpu.get_barrier_semaphore()
    peers = [sibling] + [along_z(d) for d in range(1, 8)]
    for e in (c, 1 - c):
        peers += [(x, z, lax.rem(y + d, 4), e) for d in range(1, 4)] + [(lax.rem(x + d, 4), z, y, e) for d in range(1, 4)]
    for peer in peers:
        pl.semaphore_signal(barrier, inc=1, device_id=peer, device_id_type=MESH)
    pl.semaphore_wait(barrier, len(peers))

    def dests(n, i):
        order = [lax.rem(i + n // 2, n)]
        for k in range(n // 2 - 1, 0, -1):
            order += [lax.rem(i + k, n), lax.rem(i + n - k, n)]
        return order + [i]

    def arrive(dst, sem):
        pltpu.make_async_remote_copy(
            src_ref=dst, dst_ref=dst, send_sem=sem, recv_sem=sem, device_id=sibling, device_id_type=MESH
        ).wait_recv()

    def role(core, n, i, first_axis, n2, i2, second_axis, points):
        many = 32 // n
        half = many // 2
        sends = []

        def send(src, dst, s, r, peer):
            move = pltpu.make_async_remote_copy(
                src_ref=src, dst_ref=dst, send_sem=s, recv_sem=r, device_id=peer, device_id_type=MESH
            )
            move.start()
            sends.append(move)

        def pool_along_y():
            own = pltpu.make_async_copy(p_ref.at[core, pl.ds(y * 8, 8)], pool_y.at[0], local_sem.at[8])
            own.start()
            for k in (4, 5, 2, 3, 6, 7, 1):
                d, e = k // 2, k % 2
                to, yy = core ^ e, lax.rem(y + d, 4)
                send(p_ref.at[to, pl.ds(yy * 8, 8)], pool_y.at[k], pb_send.at[k], pb_recv.at[k], (x, z, yy, to))
            return own

        def pool_along_z():
            pool_own.wait()
            total = pool_y[0]
            for k in range(1, 8):
                arrive(pool_y.at[k], pb_recv.at[k])
                total = total + pool_y[k]
            pool_z[...] = total
            for d in (4, 3, 5, 2, 6, 1, 7):
                send(pool_z.at[lax.rem(z + d, 8)], pool_zin.at[d], pc_send.at[d], pc_recv.at[d], along_z(d))

        def pool_along_x():
            total = pool_z[z]
            for d in range(1, 8):
                arrive(pool_zin.at[d], pc_recv.at[d])
                total = total + pool_zin[d]
            pool[0] = total
            for d in (2, 1, 3):
                send(pool.at[0], pool.at[d], x_send.at[d], x_recv.at[d], (lax.rem(x + d, 4), z, y, core))

        def prior_along_z():
            for d in range(1, 4):
                arrive(pool.at[d], x_recv.at[d])
            total = (pool[0] + pool[1]) + (pool[2] + pool[3])
            prior[y * 2 + core, z] = pltpu.roll(total, 4, 0) / (1.0 + total)
            for d in (4, 3, 5, 2, 6, 1, 7):
                at = prior.at[y * 2 + core, z]
                send(at, at, z_send.at[d], z_recv.at[d], along_z(d))

        def prior_along_y():
            for d in range(1, 8):
                arrive(prior.at[y * 2 + core, lax.rem(z + 8 - d, 8)], z_recv.at[d])
            for k in (4, 5, 2, 3, 6, 7, 1):
                at = prior.at[y * 2 + core]
                send(at, at, y_send.at[k], y_recv.at[k], (x, z, lax.rem(y + k // 2, 4), core ^ (k % 2)))

        pool_own = pool_along_y()
        sib_n, sib_i = (8, z) if core == 0 else (4, y)
        sib_many = 32 // sib_n
        for j, d in enumerate(dests(sib_n, sib_i)):
            at = pl.ds(d * sib_many, sib_many)
            send(g_ref.at[1 - core, at], other.at[at], s0_send.at[j], s0_recv.at[j], sibling)
        mine = []
        for j, d in enumerate(dests(n, i)):
            at = pl.ds(d * many, many)
            load = pltpu.make_async_copy(g_ref.at[core, at], part.at[at], local_sem.at[j])
            load.start()
            mine.append((load, at))
        ready = set()

        def prepare(k, way):
            j = 0 if k == n // 2 else (n - 1 if k == 0 else 1 + 2 * (n // 2 - 1 - k) + way)
            if j in ready:
                return
            ready.add(j)
            load, at = mine[j]
            load.wait()
            arrive(other.at[at], s0_recv.at[j])
            part[at] += other[at]

        def piece(d, sub):
            return part.at[pl.ds(d * many + sub * half, half)]

        def land(way, j):
            return land1.at[pl.ds((way * (n - 1) + j) * half, half)]

        def hook(j):
            if j in points:
                points[j](pool_along_z, pool_along_x, prior_along_z)

        sends += reduce_along(n, i, first_axis, piece, land, s1_send, s1_recv, prepare, hook)

        prior_along_y()
        far = sorted(range(1, n2), key=lambda d: -min(d, n2 - d))
        for d in far:
            send(part.at[i * many + lax.rem(i2 + d, n2)], land2.at[d], s2_send.at[d], s2_recv.at[d], second_axis(d))
        quarter = 2 * core + side
        grid[quarter] = part[i * many + i2]
        for d in reversed(far):
            arrive(land2.at[d], s2_recv.at[d])
            grid[quarter] += land2[d]
        for j, peer in enumerate((sibling, (x, z, pair, c), (x, z, pair, 1 - c))):
            send(grid.at[quarter], grid.at[quarter], ag_send.at[j], ag_recv.at[j], peer)
        for k in range(1, 8):
            arrive(prior.at[lax.rem(y + 4 - k // 2, 4) * 2 + (core ^ (k % 2))], y_recv.at[k])
        for j, q in enumerate((2 * (1 - core) + side, 2 * core + 1 - side, 2 * (1 - core) + 1 - side)):
            arrive(grid.at[q], ag_recv.at[j])
        for move in sends:
            move.wait_send()

    def nth(k):
        return lambda *steps: steps[k]()

    @pl.when(c == 0)
    def _():
        role(0, 4, y, along_y, 8, z, along_z, {0: nth(0), 1: nth(1), 2: nth(2)})

    @pl.when(c == 1)
    def _():
        role(1, 8, z, along_z, 4, y, along_y, {1: nth(0), 3: nth(1), 5: nth(2)})

    quarter = 2 * c + side
    t = 2 * z + y // 2
    wa, wd, cred = age_weight[t], dur_weight[t], credibility[t]
    expo = jnp.concatenate([grid[q, 0:64] for q in range(4)], 0)
    claim = jnp.concatenate([grid[q, 64:128] for q in range(4)], 0)
    diagonal = expo + cred
    under = lax.broadcasted_iota(I32, (8, 128), 0) < 4
    pooled = [
        jnp.where(under, prior[2 * yy, zz], pltpu.roll(prior[2 * yy + 1, zz], 4, 0)) for zz in range(8) for yy in range(4)
    ]
    residual = claim + cred * jnp.concatenate(pooled, 0)
    direction = residual
    smoothed = jnp.zeros_like(residual)

    def dot(a, b):
        return jnp.sum(a * b, axis=(0, 1), keepdims=True)

    norm = dot(residual, residual)
    for _ in range(ITERS):
        image = diagonal * direction + wa * penalty(direction, 1) + wd * penalty(direction, 0)
        alpha = norm / dot(direction, image)
        smoothed = smoothed + alpha * direction
        residual = residual - alpha * image
        new = dot(residual, residual)
        direction = residual + (new / norm) * direction
        norm = new
    field[0] = smoothed
    field[1] = residual

    for j in range(8):
        at = pl.ds(pl.multiple_of(quarter * 64 + j * 8, 8), 8)
        for k in range(2):
            v = field[k, at]
            done[2 * j, k] = v[0:4]
            done[2 * j + 1, k] = v[4:8]

    chip = z * 4 + y

    def result(j):
        m = quarter * 8 + j // 2
        return jnp.logical_not((m == chip) & (j % 2 == c)), pltpu.make_async_remote_copy(
            src_ref=done.at[j], dst_ref=got.at[t], send_sem=o_send.at[j], recv_sem=o_recv.at[t],
            device_id=(x, quarter * 2 + j // 8, (j // 2) % 4, j % 2), device_id_type=MESH,
        )

    for j in range(16):
        away, move = result(j)
        pl.when(away)(move.start)
    here = z // 2 == quarter

    @pl.when(here)
    def _():
        got[t] = done[lax.rem(chip, 8) * 2 + c]

    for tt in range(16):
        @pl.when(jnp.logical_not(here & (t == tt)))
        def _():
            arrive(got.at[tt], o_recv.at[tt])

    out_s[...] = got[:, 0]
    out_r[...] = got[:, 1]
    for j in range(16):
        away, move = result(j)
        pl.when(away)(move.wait_send)


def smooth(parts, pooled, smooth_age, smooth_dur, credibility):
    smem = pl.BlockSpec(memory_space=pltpu.SMEM)
    vmem = pl.BlockSpec(memory_space=pltpu.VMEM)
    whole = pl.BlockSpec(memory_space=pl.ANY)
    dma = pltpu.SemaphoreType.DMA
    return pl.pallas_call(
        smooth_kernel,
        out_shape=(jax.ShapeDtypeStruct((16, 4, 128), F32),) * 2,
        in_specs=[whole, whole, smem, smem, smem],
        out_specs=(vmem, vmem),
        scratch_shapes=[
            pltpu.VMEM((32, 128, 128), F32),
            pltpu.VMEM((32, 128, 128), F32),
            pltpu.VMEM((28, 128, 128), F32),
            pltpu.VMEM((8, 128, 128), F32),
            pltpu.VMEM((4, 128, 128), F32),
            pltpu.VMEM((8, 8, 8, 128), F32),
            pltpu.VMEM((8, 8, 128), F32),
            pltpu.VMEM((8, 8, 128), F32),
            pltpu.VMEM((8, 8, 128), F32),
            pltpu.VMEM((8, 8, 8, 128), F32),
            pltpu.VMEM((2, 256, 128), F32),
            pltpu.VMEM((16, 2, 4, 128), F32),
            pltpu.VMEM((16, 2, 4, 128), F32),
            dma((9,)), dma((8,)), dma((8,)),
            dma((2, 7)), dma((2, 7)), dma((8,)), dma((8,)), dma((3,)), dma((3,)),
            dma((8,)), dma((8,)), dma((8,)), dma((8,)), dma((8,)), dma((8,)),
            dma((8,)), dma((8,)), dma((8,)), dma((8,)), dma((16,)), dma((16,)),
        ],
        compiler_params=pltpu.CompilerParams(collective_id=0, has_side_effects=True, vmem_limit_bytes=(64 << 20) - (200 << 10)),
        cost_estimate=pl.CostEstimate(flops=20 << 20, bytes_accessed=6 << 20, transcendentals=0),
        name="reduce_and_smooth",
    )(parts, pooled, smooth_age, smooth_dur, credibility)


def per_device(
    age_cell, dur_cell, trans_code, age_frac, dur_frac, exposure, claims, block_tile, smooth_age, smooth_dur, credibility
):
    fields = [
        f.reshape(-1, 128) for f in (age_cell, dur_cell, trans_code, age_frac, dur_frac, exposure, claims)
    ]
    parts, pooled = grids(block_tile.reshape(-1), fields)
    return smooth(parts, pooled, smooth_age, smooth_dur, credibility)


def solution(mesh):
    split = Mesh(mesh.devices.reshape(mesh.shape["tg"], 8, 4, 2), ("tg", "z", "y", "c"))
    tile = ("z", "y", "c")
    placed = (P("tg", tile),) * 7 + (P("tg", tile, None),) + (P("tg"),) * 3
    return jax.shard_map(
        per_device,
        mesh=split,
        in_specs=placed,
        out_specs=(P("tg", tile, None),) * 2,
        check_vma=False,
    )
```

```python
import jax, jax.numpy as jnp
from jax import lax
from jax.experimental import pallas as pl
from jax.experimental.pallas import tpu as pltpu
from jax.sharding import Mesh
from jax.sharding import PartitionSpec as P

ITERS = 4
MESH = pl.DeviceIdType.MESH
HBM = pltpu.MemorySpace.HBM
F32, BF16, I32 = jnp.float32, jnp.bfloat16, jnp.int32

def spline(f):
    r = 1.0 - f
    f2 = f * f
    c = f2 * f
    s = 1.0 / 6.0
    return (r * r * r * s, (3.0 * c - 6.0 * f2 + 4.0) * s, (-3.0 * c + 3.0 * f2 + 3.0 * f + 1.0) * s, c * s)

def grid_kernel(
    tile_ref, age_hbm, dur_hbm, code_hbm, af_hbm, df_hbm, ex_hbm, cl_hbm, out_hbm, pool_hbm,
    acc, age_ref, dur_ref, code_ref, af_ref, df_ref, ex_ref, cl_ref, weights, out_ref, pool_ref, sem, out_sem,
):
    pairs = (
        (age_hbm, age_ref), (dur_hbm, dur_ref), (code_hbm, code_ref), (af_hbm, af_ref),
        (df_hbm, df_ref), (ex_hbm, ex_ref), (cl_hbm, cl_ref),
    )

    def loads(part):
        at = pl.ds(part * 128, 128)
        return [pltpu.make_async_copy(src.at[at], dst.at[at], sem.at[part, k]) for k, (src, dst) in enumerate(pairs)]

    for part in range(4):
        for load in loads(part):
            load.start()
    acc[...] = jnp.zeros(acc.shape, F32)
    iota8 = lax.broadcasted_iota(I32, (8, 128), 0)
    iota16 = lax.broadcasted_iota(I32, (16, 128), 0)
    half16 = (iota16 >> 3).astype(F32).astype(BF16)
    zero16 = jnp.zeros((16, 128), BF16)
    r1 = iota16 + 1

    def twice(v):
        return jnp.concatenate([v, v], 0)

    def group(g, slot):
        base = pl.multiple_of(g * 8, 8)
        at = pl.ds(base, 8)
        for k, v in enumerate(spline(af_ref[at, :]) + spline(df_ref[at, :])):
            weights[slot, k] = v
        for i in range(8):
            def row(ref):
                return ref[pl.ds(base + i, 8, stride=0), :]

            def weight(k):
                return weights[slot, k, pl.ds(i, 8, stride=0), :]

            delta = iota8 - row(dur_ref)
            w = jnp.where(delta == 0, weight(4), 0.0)
            for k in range(1, 4):
                w = jnp.where(delta == k, weight(4 + k), w)
            e16 = twice(w * row(ex_ref)).astype(BF16)
            c16 = twice(w * row(cl_ref)).astype(BF16)
            code = twice(row(code_ref)).astype(F32).astype(BF16) - half16
            left_e, left_c = [], []
            for j in range(8):
                m = code == jnp.bfloat16(2 * j)
                left_e.append(jnp.where(m, e16, zero16))
                left_c.append(jnp.where(m, c16, zero16))
            left = jnp.concatenate(left_e + left_c, 0)
            age = twice(row(age_ref))
            kk = (r1 - age) & 15
            a = jnp.where(kk == 0, twice(weight(0)), 0.0)
            for k in range(1, 4):
                a = jnp.where(kk == k, twice(weight(k)), a)
            a16 = a.astype(BF16)
            block = ((age - 1 + kk) >> 4).astype(F32).astype(BF16)
            right = jnp.concatenate([jnp.where(block == jnp.bfloat16(q), a16, zero16) for q in range(8)], 0)
            res = lax.dot_general(left, right, (((1,), (1,)), ((), ())), preferred_element_type=F32)
            tile = tile_ref[g * 8 + i]
            acc[(tile & 1) * 32 + (tile >> 1)] += res

    def groups(step, carry):
        for slot in range(8):
            group(step * 8 + slot, slot)
        return carry

    def quarter(part, carry):
        for load in loads(part):
            load.wait()
        return lax.fori_loop(part * 2, part * 2 + 2, groups, carry)

    lax.fori_loop(0, 4, quarter, 0)

    low = iota8 < 4
    stores = []

    def joined(m, h, s):
        r8 = pl.multiple_of(lax.rem(m, 8) * 8, 8)
        up = jnp.minimum(m + 1, 31)
        dn = jnp.maximum(m - 1, 0)
        end = (iota8 == 0) & (m == 31)
        begin = (iota8 >= 5) & (m == 0)
        pooled = []
        for ch in range(2):
            total = jnp.zeros((8, 128), F32)
            for t in range(16):
                sl = pl.ds((ch * 16 + t) * 8, 8)
                ev = jnp.where(iota8 == 0, acc[up, sl, :], acc[m, sl, :])
                ev = pltpu.roll(jnp.where(end, 0.0, ev), 7, 0)
                od = jnp.where(iota8 >= 5, acc[32 + dn, sl, :], acc[32 + m, sl, :])
                v = ev + pltpu.roll(jnp.where(begin, 0.0, od), 3, 0)
                total = total + v
                z, y = t >> 1, 2 * (t & 1) + s
                out_ref[h, y * 8 + z if h == 0 else z * 4 + y, pl.ds(ch * 64 + r8, 8), :] = v
            pooled.append(total)
        pe, po = pooled
        at = lax.rem(m, 4) * 8 + m // 4
        pool_ref[0, at] = jnp.where(low, pe, pltpu.roll(po, 4, 0))
        pool_ref[1, at] = jnp.where(low, pltpu.roll(pe, 4, 0), po)

    for h in range(2):
        for s in range(2):
            first = h * 16 + s * 8

            def some(step, carry):
                for k in range(4):
                    joined(first + step * 4 + k, h, s)
                return carry

            lax.fori_loop(0, 2, some, 0)
            if h == 0:
                slots = [pl.ds(y * 8, 8) for y in (s, s + 2)]
            else:
                slots = [z * 4 + y for z in range(8) for y in (s, s + 2)]
            for k, at in enumerate(slots):
                stores.append(pltpu.make_async_copy(out_ref.at[h, at], out_hbm.at[h, at], out_sem.at[h * 2 + s, k]))
                stores[-1].start()
    stores.append(pltpu.make_async_copy(pool_ref, pool_hbm, out_sem.at[4, 0]))
    stores[-1].start()
    for store in stores:
        store.wait()


def grids(tiles, fields):
    whole = pl.BlockSpec(memory_space=HBM)
    return pl.pallas_call(
        grid_kernel,
        out_shape=(
            jax.ShapeDtypeStruct((2, 32, 128, 128), F32),
            jax.ShapeDtypeStruct((2, 32, 8, 128), F32),
        ),
        in_specs=[pl.BlockSpec(memory_space=pltpu.SMEM)] + [whole] * 7,
        out_specs=(whole, whole),
        scratch_shapes=[pltpu.VMEM((64, 256, 128), F32)]
        + [pltpu.VMEM((512, 128), I32)] * 3
        + [pltpu.VMEM((512, 128), F32)] * 4
        + [
            pltpu.VMEM((8, 8, 8, 128), F32),
            pltpu.VMEM((2, 32, 128, 128), F32),
            pltpu.VMEM((2, 32, 8, 128), F32),
            pltpu.SemaphoreType.DMA((4, 7)),
            pltpu.SemaphoreType.DMA((5, 16)),
        ],
        compiler_params=pltpu.CompilerParams(vmem_limit_bytes=63 << 20),
        cost_estimate=pl.CostEstimate(flops=2 * 512 * 256 * 128 * 128, bytes_accessed=6 << 20, transcendentals=0),
        name="local_grid",
    )(tiles, *fields)


def penalty(v, axis):
    n = v.shape[axis]
    place = lax.broadcasted_iota(I32, v.shape, axis)
    u = v - 2.0 * pltpu.roll(v, n - 1, axis) + pltpu.roll(v, n - 2, axis)
    u = jnp.where(place < n - 2, u, 0.0)
    return u - 2.0 * pltpu.roll(u, 1, axis) + pltpu.roll(u, 2, axis)


def chain_order(n):
    order = [(n // 2, 0)]
    for k in range(n // 2 - 1, 0, -1):
        order += [(k, 1), (k, 0)]
    return order


def reduce_along(n, me, neighbour, piece, land, send_sem, recv_sem, prepare, hook):
    order = chain_order(n)
    started = []

    def half_of(way, j):
        return order[j][1] if way == 0 else 1 - order[j][1]

    def transfer(way, j):
        k, _ = order[j]
        sub = half_of(way, j)
        dest = lax.rem(me + (k if way == 0 else n - k), n)
        return pltpu.make_async_remote_copy(
            src_ref=piece(dest, sub),
            dst_ref=land(way, j),
            send_sem=send_sem.at[way, j],
            recv_sem=recv_sem.at[way, j],
            device_id=neighbour(1 if way == 0 else n - 1),
            device_id_type=MESH,
        )

    def take(way, j, dest):
        transfer(way, j).wait_recv()
        target = piece(dest, half_of(way, j))
        target[...] += land(way, j)[...]

    for j, (k, first) in enumerate(order):
        for way in (0, 1):
            prepare(k, way)
            if (k + 1, first) in order:
                take(way, order.index((k + 1, first)), lax.rem(me + (k if way == 0 else n - k), n))
            move = transfer(way, j)
            move.start()
            started.append(move)
        hook(j)
    prepare(0, 0)
    for first in (1, 0):
        for way in (0, 1):
            take(way, order.index((1, first)), me)
    return started


def smooth_kernel(
    g_ref, p_ref, age_weight, dur_weight, credibility, out_s, out_r,
    part, other, land1, land2, grid, pool_y, pool_z, pool_zin, pool, prior, field, done, got,
    local_sem, s0_send, s0_recv, s1_send, s1_recv, s2_send, s2_recv, ag_send, ag_recv,
    pb_send, pb_recv, pc_send, pc_recv, x_send, x_recv, y_send, y_recv, z_send, z_recv, o_send, o_recv,
):
    x, z, y, c = (lax.axis_index(a) for a in ("tg", "z", "y", "c"))
    sibling = (x, z, y, 1 - c)
    side = lax.rem(y, 2)
    pair = y + 1 - 2 * side

    def along_y(d):
        return (x, z, lax.rem(y + d, 4), c)

    def along_z(d):
        return (x, lax.rem(z + d, 8), y, c)

    barrier = pltpu.get_barrier_semaphore()
    peers = [sibling] + [along_z(d) for d in range(1, 8)]
    for e in (c, 1 - c):
        peers += [(x, z, lax.rem(y + d, 4), e) for d in range(1, 4)] + [(lax.rem(x + d, 4), z, y, e) for d in range(1, 4)]
    for peer in peers:
        pl.semaphore_signal(barrier, inc=1, device_id=peer, device_id_type=MESH)
    pl.semaphore_wait(barrier, len(peers))

    def dests(n, i):
        order = [lax.rem(i + n // 2, n)]
        for k in range(n // 2 - 1, 0, -1):
            order += [lax.rem(i + k, n), lax.rem(i + n - k, n)]
        return order + [i]

    def arrive(dst, sem):
        pltpu.make_async_remote_copy(
            src_ref=dst, dst_ref=dst, send_sem=sem, recv_sem=sem, device_id=sibling, device_id_type=MESH
        ).wait_recv()

    def role(core, n, i, first_axis, n2, i2, second_axis, points):
        many = 32 // n
        half = many // 2
        sends = []

        def send(src, dst, s, r, peer):
            move = pltpu.make_async_remote_copy(
                src_ref=src, dst_ref=dst, send_sem=s, recv_sem=r, device_id=peer, device_id_type=MESH
            )
            move.start()
            sends.append(move)

        def pool_along_y():
            own = pltpu.make_async_copy(p_ref.at[core, pl.ds(y * 8, 8)], pool_y.at[0], local_sem.at[8])
            own.start()
            for k in (4, 5, 2, 3, 6, 7, 1):
                d, e = k // 2, k % 2
                to, yy = core ^ e, lax.rem(y + d, 4)
                send(p_ref.at[to, pl.ds(yy * 8, 8)], pool_y.at[k], pb_send.at[k], pb_recv.at[k], (x, z, yy, to))
            return own

        def pool_along_z():
            pool_own.wait()
            total = pool_y[0]
            for k in range(1, 8):
                arrive(pool_y.at[k], pb_recv.at[k])
                total = total + pool_y[k]
            pool_z[...] = total
            for d in (4, 3, 5, 2, 6, 1, 7):
                send(pool_z.at[lax.rem(z + d, 8)], pool_zin.at[d], pc_send.at[d], pc_recv.at[d], along_z(d))

        def pool_along_x():
            total = pool_z[z]
            for d in range(1, 8):
                arrive(pool_zin.at[d], pc_recv.at[d])
                total = total + pool_zin[d]
            pool[0] = total
            for d in (2, 1, 3):
                send(pool.at[0], pool.at[d], x_send.at[d], x_recv.at[d], (lax.rem(x + d, 4), z, y, core))

        def prior_along_z():
            for d in range(1, 4):
                arrive(pool.at[d], x_recv.at[d])
            total = (pool[0] + pool[1]) + (pool[2] + pool[3])
            prior[y * 2 + core, z] = pltpu.roll(total, 4, 0) / (1.0 + total)
            for d in (4, 3, 5, 2, 6, 1, 7):
                at = prior.at[y * 2 + core, z]
                send(at, at, z_send.at[d], z_recv.at[d], along_z(d))

        def prior_along_y():
            for d in range(1, 8):
                arrive(prior.at[y * 2 + core, lax.rem(z + 8 - d, 8)], z_recv.at[d])
            for k in (4, 5, 2, 3, 6, 7, 1):
                at = prior.at[y * 2 + core]
                send(at, at, y_send.at[k], y_recv.at[k], (x, z, lax.rem(y + k // 2, 4), core ^ (k % 2)))

        pool_own = pool_along_y()
        sib_n, sib_i = (8, z) if core == 0 else (4, y)
        sib_many = 32 // sib_n
        for j, d in enumerate(dests(sib_n, sib_i)):
            at = pl.ds(d * sib_many, sib_many)
            send(g_ref.at[1 - core, at], other.at[at], s0_send.at[j], s0_recv.at[j], sibling)
        mine = []
        for j, d in enumerate(dests(n, i)):
            at = pl.ds(d * many, many)
            load = pltpu.make_async_copy(g_ref.at[core, at], part.at[at], local_sem.at[j])
            load.start()
            mine.append((load, at))
        ready = set()

        def prepare(k, way):
            j = 0 if k == n // 2 else (n - 1 if k == 0 else 1 + 2 * (n // 2 - 1 - k) + way)
            if j in ready:
                return
            ready.add(j)
            load, at = mine[j]
            load.wait()
            arrive(other.at[at], s0_recv.at[j])
            part[at] += other[at]

        def piece(d, sub):
            return part.at[pl.ds(d * many + sub * half, half)]

        def land(way, j):
            return land1.at[pl.ds((way * (n - 1) + j) * half, half)]

        def hook(j):
            if j in points:
                points[j](pool_along_z, pool_along_x, prior_along_z)

        sends += reduce_along(n, i, first_axis, piece, land, s1_send, s1_recv, prepare, hook)

        far = sorted(range(1, n2), key=lambda d: -min(d, n2 - d))
        for d in far:
            send(part.at[i * many + lax.rem(i2 + d, n2)], land2.at[d], s2_send.at[d], s2_recv.at[d], second_axis(d))
        if len(points) < 3:
            prior_along_z()
        prior_along_y()
        quarter = 2 * core + side
        grid[quarter] = part[i * many + i2]
        for d in reversed(far):
            arrive(land2.at[d], s2_recv.at[d])
            grid[quarter] += land2[d]
        for j, peer in enumerate((sibling, (x, z, pair, c), (x, z, pair, 1 - c))):
            send(grid.at[quarter], grid.at[quarter], ag_send.at[j], ag_recv.at[j], peer)
        for k in range(1, 8):
            arrive(prior.at[lax.rem(y + 4 - k // 2, 4) * 2 + (core ^ (k % 2))], y_recv.at[k])
        for j, q in enumerate((2 * (1 - core) + side, 2 * core + 1 - side, 2 * (1 - core) + 1 - side)):
            arrive(grid.at[q], ag_recv.at[j])
        for move in sends:
            move.wait_send()

    def nth(k):
        return lambda *steps: steps[k]()

    @pl.when(c == 0)
    def _():
        role(0, 4, y, along_y, 8, z, along_z, {0: nth(0), 2: nth(1)})

    @pl.when(c == 1)
    def _():
        role(1, 8, z, along_z, 4, y, along_y, {1: nth(0), 4: nth(1), 6: nth(2)})

    quarter = 2 * c + side
    t = 2 * z + y // 2
    wa, wd, cred = age_weight[t], dur_weight[t], credibility[t]
    expo = jnp.concatenate([grid[q, 0:64] for q in range(4)], 0)
    claim = jnp.concatenate([grid[q, 64:128] for q in range(4)], 0)
    diagonal = expo + cred
    under = lax.broadcasted_iota(I32, (8, 128), 0) < 4
    pooled = [
        jnp.where(under, prior[2 * yy, zz], pltpu.roll(prior[2 * yy + 1, zz], 4, 0)) for zz in range(8) for yy in range(4)
    ]
    residual = claim + cred * jnp.concatenate(pooled, 0)
    direction = residual
    smoothed = jnp.zeros_like(residual)

    def dot(a, b):
        return jnp.sum(a * b, axis=(0, 1), keepdims=True)

    norm = dot(residual, residual)
    for _ in range(ITERS):
        image = diagonal * direction + wa * penalty(direction, 1) + wd * penalty(direction, 0)
        alpha = norm / dot(direction, image)
        smoothed = smoothed + alpha * direction
        residual = residual - alpha * image
        new = dot(residual, residual)
        direction = residual + (new / norm) * direction
        norm = new
    field[0] = smoothed
    field[1] = residual

    for j in range(8):
        at = pl.ds(pl.multiple_of(quarter * 64 + j * 8, 8), 8)
        for k in range(2):
            v = field[k, at]
            done[2 * j, k] = v[0:4]
            done[2 * j + 1, k] = v[4:8]

    chip = z * 4 + y

    def result(j):
        m = quarter * 8 + j // 2
        return jnp.logical_not((m == chip) & (j % 2 == c)), pltpu.make_async_remote_copy(
            src_ref=done.at[j], dst_ref=got.at[t], send_sem=o_send.at[j], recv_sem=o_recv.at[t],
            device_id=(x, quarter * 2 + j // 8, (j // 2) % 4, j % 2), device_id_type=MESH,
        )

    for j in range(16):
        away, move = result(j)
        pl.when(away)(move.start)
    here = z // 2 == quarter

    @pl.when(here)
    def _():
        got[t] = done[lax.rem(chip, 8) * 2 + c]

    for tt in range(16):
        @pl.when(jnp.logical_not(here & (t == tt)))
        def _():
            arrive(got.at[tt], o_recv.at[tt])

    out_s[...] = got[:, 0]
    out_r[...] = got[:, 1]
    for j in range(16):
        away, move = result(j)
        pl.when(away)(move.wait_send)


def smooth(parts, pooled, smooth_age, smooth_dur, credibility):
    smem = pl.BlockSpec(memory_space=pltpu.SMEM)
    vmem = pl.BlockSpec(memory_space=pltpu.VMEM)
    whole = pl.BlockSpec(memory_space=pl.ANY)
    dma = pltpu.SemaphoreType.DMA
    return pl.pallas_call(
        smooth_kernel,
        out_shape=(jax.ShapeDtypeStruct((16, 4, 128), F32),) * 2,
        in_specs=[whole, whole, smem, smem, smem],
        out_specs=(vmem, vmem),
        scratch_shapes=[
            pltpu.VMEM((32, 128, 128), F32),
            pltpu.VMEM((32, 128, 128), F32),
            pltpu.VMEM((28, 128, 128), F32),
            pltpu.VMEM((8, 128, 128), F32),
            pltpu.VMEM((4, 128, 128), F32),
            pltpu.VMEM((8, 8, 8, 128), F32),
            pltpu.VMEM((8, 8, 128), F32),
            pltpu.VMEM((8, 8, 128), F32),
            pltpu.VMEM((8, 8, 128), F32),
            pltpu.VMEM((8, 8, 8, 128), F32),
            pltpu.VMEM((2, 256, 128), F32),
            pltpu.VMEM((16, 2, 4, 128), F32),
            pltpu.VMEM((16, 2, 4, 128), F32),
            dma((9,)), dma((8,)), dma((8,)),
            dma((2, 7)), dma((2, 7)), dma((8,)), dma((8,)), dma((3,)), dma((3,)),
            dma((8,)), dma((8,)), dma((8,)), dma((8,)), dma((8,)), dma((8,)),
            dma((8,)), dma((8,)), dma((8,)), dma((8,)), dma((16,)), dma((16,)),
        ],
        compiler_params=pltpu.CompilerParams(collective_id=0, has_side_effects=True, vmem_limit_bytes=(64 << 20) - (200 << 10)),
        cost_estimate=pl.CostEstimate(flops=20 << 20, bytes_accessed=6 << 20, transcendentals=0),
        name="reduce_and_smooth",
    )(parts, pooled, smooth_age, smooth_dur, credibility)


def per_device(
    age_cell, dur_cell, trans_code, age_frac, dur_frac, exposure, claims, block_tile, smooth_age, smooth_dur, credibility
):
    fields = [
        f.reshape(-1, 128) for f in (age_cell, dur_cell, trans_code, age_frac, dur_frac, exposure, claims)
    ]
    parts, pooled = grids(block_tile.reshape(-1), fields)
    return smooth(parts, pooled, smooth_age, smooth_dur, credibility)


def solution(mesh):
    split = Mesh(mesh.devices.reshape(mesh.shape["tg"], 8, 4, 2), ("tg", "z", "y", "c"))
    tile = ("z", "y", "c")
    placed = (P("tg", tile),) * 7 + (P("tg", tile, None),) + (P("tg"),) * 3
    return jax.shard_map(
        per_device,
        mesh=split,
        in_specs=placed,
        out_specs=(P("tg", tile, None),) * 2,
        check_vma=False,
    )
```
